32 devices in a mesh: dp: 8 (over z, y), head: 4 (over x, core).
Axes of the slice: x: 2, y: 2, z: 4, core: 2. Of those that a mesh axis runs over, the one named last changes fastest.
Arguments:
- latent: bfloat16 [12288, 512], P('dp', 'head'), may hold values from -6 to 6
- value_grad: bfloat16 [12288, 2048], P('dp', 'head'), may hold values from -6 to 6
- lengths: int32 [8], replicated, may hold values from 1 to 1536, 4096 in all
Outputs:
- update: bfloat16 [16, 512, 128], P('head')
The draws below stay inside these ranges and needn't reach their ends.
Inputs may be any that keep to these rules, and one draw needn't show every extreme that they name: The lengths sum to 4096; the longest is exactly 1536.
All inputs are finite; a program needn't handle non-finite values.
Results may differ from the reference program's by a relative error of at most 0.035.
Values may be sent and summed in bfloat16 or wider, within the bound.
A program may use at most 64 MiB of HBM per device.

```python
import math
import jax
import jax.numpy as jnp
import numpy as np
from jax import lax

KV_RANK = 512
V_DIM = 128
HEADS = 16
MEAN_LEN = 512
ITERS = 5
CAP = 1536
ROWS = 12288
N_DP = 8


def strengthened(values, rng, source, target, blocks, factor):
    def block_of(axis_at):
        return (jnp.arange(values.shape[axis_at]) // (values.shape[axis_at] // blocks)).reshape((-1,) + (1,) * (values.ndim - 1 - axis_at))

    first = jax.random.permutation(rng, blocks)[block_of(target)]
    second = (block_of(target) + blocks // 2) % blocks
    return jnp.where((block_of(source) == first) | (block_of(source) == second), factor * values, values)


def levels(stream_key, shape, shards, smallest, largest):
    factor_of, own = 1.0, jax.random.fold_in(stream_key, 6)
    for axis_at, shards_of in shards:
        draws = jnp.exp(jax.random.uniform(jax.random.fold_in(own, axis_at), (shards_of,), jnp.float32, smallest / len(shards), largest / len(shards)))
        factor_of = factor_of * jnp.repeat(draws, shape[axis_at] // shards_of).reshape([-1 if axis == axis_at else 1 for axis in range(len(shape))])
    return factor_of


def profile(amount, total, most, lean):
    portions = [(1 << 20) // math.isqrt(standing ** lean) + 1 for standing in range(2, amount + 1)]
    spare, counts = total - most - (amount - 1), [1] * (amount - 1)
    while spare > 0:
        candidates = [i for i in range(amount - 1) if counts[i] < most]
        pool, budget = sum([portions[i] for i in candidates]), spare
        for i in candidates:
            addition = min(most - counts[i], max(1, budget * portions[i] // pool), spare)
            counts[i] = counts[i] + addition
            spare = spare - addition
    return np.array([most] + counts)


def ragged_sizes(stream_key, amount, total, most, slope):
    if amount == 2:
        one = jax.random.randint(stream_key, (), max(1, total - most), min(most, total - 1) + 1)
        return jnp.stack([one, total - one])
    sizes = jnp.asarray(profile(amount, total, most, slope), jnp.int32)
    twos = (amount - 1) // 2
    donor, receiver = sizes[1:1 + 2 * twos:2], sizes[2:2 + 2 * twos:2]
    slack = jnp.minimum(donor - 1, most - receiver)
    shifted = jax.random.randint(jax.random.fold_in(stream_key, 1), (twos,), 0, 1 << 20) % (slack + 1)
    sizes = sizes.at[1:1 + 2 * twos:2].set(donor - shifted).at[2:2 + 2 * twos:2].set(receiver + shifted)
    return sizes[jax.random.permutation(jax.random.fold_in(stream_key, 2), amount)]


def normal_values(stream_key, extent, width, limit, shards=(), kind=jnp.bfloat16):
    values = width * jax.random.normal(stream_key, extent, jnp.float32)
    if shards:
        values = values * levels(stream_key, extent, shards, -0.22, 0.18)
    return jnp.clip(values, -limit, limit).astype(kind)


def heavy_noise(own_key, shape, width, bound, pieces, heavy, held_as=jnp.bfloat16):
    drawn = width * jax.random.normal(own_key, shape, jnp.float32)
    if pieces:
        drawn = drawn * levels(own_key, shape, pieces, -0.22, 0.18)
    return jnp.clip(strengthened(drawn, jax.random.fold_in(own_key, 3), *heavy), -bound, bound).astype(held_as)


def setup_inputs(seed: int = 0) -> dict:
    seeds = jax.random.split(jax.random.key(seed), 4)
    latent = heavy_noise(seeds[0], (ROWS, KV_RANK), 1.0, 6.0, ((0, 8), (1, 4)), (0, 1, 8, 2.0))
    value_grad = normal_values(seeds[1], (ROWS, HEADS * V_DIM), 1.0, 6.0, ((0, 8), (1, 4)))
    lengths = ragged_sizes(seeds[2], N_DP, N_DP * MEAN_LEN, CAP, 2).astype(jnp.int32)
    return {"latent": latent, "value_grad": value_grad, "lengths": lengths}


epsilon = 1e-07
coef_one = 3.4445
coef_two = -4.775
coef_three = 2.0315

def newton_schulz(grad_sum):
    split = grad_sum.reshape(KV_RANK, HEADS, V_DIM)
    head_squares = lax.optimization_barrier(jnp.sum(split * split, axis=(0, 2)))
    head_norm = jnp.sqrt(head_squares)
    ortho = (split / (head_norm[None, :, None] + epsilon)).astype(jnp.bfloat16)
    for step in range(ITERS):
        wide = ortho.astype(jnp.float32)
        gram_mat = jnp.einsum('rhv,rhw->hvw', wide, wide, precision=lax.Precision.HIGHEST).astype(jnp.bfloat16)
        gram_wide = gram_mat.astype(jnp.float32)
        squared = jnp.einsum('hvu,huw->hvw', gram_wide, gram_wide, precision=lax.Precision.HIGHEST)
        poly_mat = (coef_two * gram_wide + coef_three * squared).astype(jnp.bfloat16)
        product = jnp.einsum('rhv,hvw->rhw', wide, poly_mat.astype(jnp.float32), precision=lax.Precision.HIGHEST)
        ortho = (coef_one * wide + product).astype(jnp.bfloat16)
    scale = 0.2 * max(KV_RANK, V_DIM) ** 0.5
    update = (scale * ortho.astype(jnp.float32)).astype(jnp.bfloat16)
    return jnp.transpose(update, (1, 0, 2))

def reference(latent, value_grad, lengths):
    row_total = latent.shape[0]
    capacity = row_total // N_DP
    positions = jnp.arange(row_total, dtype=jnp.int32)
    owner_len = jnp.repeat(lengths, capacity)
    live_rows = positions % capacity < owner_len
    masked = jnp.where(live_rows[:, None], value_grad, jnp.zeros_like(value_grad))
    grad_sum = jnp.dot(latent.T, masked, preferred_element_type=jnp.float32)
    return newton_schulz(grad_sum)
```

```python
import functools

import jax
import jax.numpy as jnp
from jax import lax
from jax.experimental import pallas as pl
from jax.experimental.pallas import tpu as pltpu
from jax.sharding import PartitionSpec as P

KV_RANK = 512
V_DIM = 128
ITERS = 5
TILE = 16
CHUNKS = 3

epsilon = 1e-07
coef_one = 3.4445
coef_two = -4.775
coef_three = 2.0315


def plain_body(latent, value_grad, lengths):
    capacity, lat_cols = latent.shape
    grad_width = value_grad.shape[1]
    head_count = grad_width // V_DIM
    my_index = lax.axis_index("dp")
    own_length = lengths[my_index]
    slot_live = jnp.arange(capacity, dtype=jnp.int32) < own_length
    rows_grad = jnp.where(slot_live[:, None], value_grad, jnp.zeros_like(value_grad))
    partial_sum = lax.dot_general(
        lax.all_gather(latent, "head", axis=1, tiled=True),
        rows_grad,
        (((0,), (0,)), ((), ())),
        preferred_element_type=jnp.float32,
    )
    dw_shard = lax.psum_scatter(partial_sum, "dp", scatter_dimension=0, tiled=True)
    shard_heads = dw_shard.reshape(dw_shard.shape[0], head_count, V_DIM)
    local_squares = jnp.sum(shard_heads * shard_heads, axis=(0, 2))
    square_total = lax.psum(local_squares, "dp")
    head_norm = jnp.sqrt(square_total)
    ortho_shard = (shard_heads / (head_norm[None, :, None] + epsilon)).astype(jnp.bfloat16)
    ortho = lax.all_gather(ortho_shard, "dp", axis=0, tiled=True)
    for step in range(ITERS):
        gram_mat = jnp.einsum(
            "rhv,rhw->hvw", ortho, ortho, preferred_element_type=jnp.float32
        ).astype(jnp.bfloat16)
        squared = jnp.einsum("hvu,huw->hvw", gram_mat, gram_mat, preferred_element_type=jnp.float32)
        poly_mat = (coef_two * gram_mat.astype(jnp.float32) + coef_three * squared).astype(
            jnp.bfloat16
        )
        product = jnp.einsum("rhv,hvw->rhw", ortho, poly_mat, preferred_element_type=jnp.float32)
        ortho = (coef_one * ortho.astype(jnp.float32) + product).astype(jnp.bfloat16)
    scale = 0.2 * max(KV_RANK, V_DIM) ** 0.5
    update = (scale * ortho.astype(jnp.float32)).astype(jnp.bfloat16)
    return jnp.transpose(update, (1, 0, 2))


def dot_f32(a, b, dims):
    return lax.dot_general(a, b, (dims, ((), ())), preferred_element_type=jnp.float32)


def newton_schulz(grads):
    final = 0.2 * max(KV_RANK, V_DIM) ** 0.5
    xs = list(grads)
    inv = []
    for g in xs:
        w = g.astype(jnp.float32)
        rows = jnp.sum(w * w, axis=0, keepdims=True)
        inv.append(1.0 / (jnp.sqrt(jnp.sum(rows, axis=1, keepdims=True)) + epsilon))
    for step in range(ITERS):
        grams = [dot_f32(x, x, ((0,), (0,))) for x in xs]
        if step == 0:
            grams = [a * s * s for a, s in zip(grams, inv)]
        grams = [a.astype(jnp.bfloat16) for a in grams]
        squares = [dot_f32(a, a, ((1,), (0,))) for a in grams]
        polys = [
            (coef_two * a.astype(jnp.float32) + coef_three * q).astype(jnp.bfloat16)
            for a, q in zip(grams, squares)
        ]
        prods = [dot_f32(x, b, ((1,), (0,))) for x, b in zip(xs, polys)]
        wide = [coef_one * x.astype(jnp.float32) + p for x, p in zip(xs, prods)]
        if step == 0:
            wide = [x * s for x, s in zip(wide, inv)]
        xs = [x.astype(jnp.bfloat16) for x in wide]
    return [(final * x.astype(jnp.float32)).astype(jnp.bfloat16) for x in xs]


def kernel(
    n_dp,
    len_ref, lat_hbm, vg_hbm, out_ref,
    lat_v, vg_v, lat_t, acc, part, rs_buf, grad,
    load_sem, sib_sem, x_send, x_recv, f_send, f_recv, rs_send, rs_recv, ag_send, ag_recv,
):
    dp = lax.axis_index("dp")
    head = lax.axis_index("head")
    core = lax.rem(head, 2)
    sibling = head + 1 - 2 * core
    partner = lax.rem(head + 2, 4)
    far = lax.rem(sibling + 2, 4)
    source = (head, sibling, partner, far)
    lat_cols, capacity = lat_t.shape[1], lat_t.shape[2]
    span = capacity // CHUNKS

    load_lat = pltpu.make_async_copy(lat_hbm, lat_v, load_sem.at[0])
    load_vg = pltpu.make_async_copy(vg_hbm, vg_v, load_sem.at[1])
    load_lat.start()
    load_vg.start()

    def peer(d):
        return lax.rem(dp + d, n_dp)

    barrier = pltpu.get_barrier_semaphore()
    for h in (sibling, partner):
        pl.semaphore_signal(barrier, inc=1, device_id=(dp, h), device_id_type=pl.DeviceIdType.MESH)
    for d in range(1, n_dp):
        pl.semaphore_signal(barrier, inc=1, device_id=(peer(d), head), device_id_type=pl.DeviceIdType.MESH)

    load_lat.wait()
    live = lax.broadcasted_iota(jnp.int32, (lat_cols, capacity), 1) < len_ref[dp]
    turned = lat_v[...].T
    lat_t[0] = jnp.where(live, turned, jnp.zeros_like(turned))
    pl.semaphore_wait(barrier, n_dp + 1)

    def remote(src, dst, ssem, rsem, where):
        return pltpu.make_async_remote_copy(
            src_ref=src, dst_ref=dst, send_sem=ssem, recv_sem=rsem,
            device_id=where, device_id_type=pl.DeviceIdType.MESH,
        )

    def cut(k):
        return pl.ds(k * span, span)

    over = [
        remote(lat_t.at[0, :, cut(k)], lat_t.at[2, :, cut(k)], x_send.at[k], x_recv.at[k], (dp, partner))
        for k in range(CHUNKS)
    ]
    forward = [
        remote(lat_t.at[2, :, cut(k)], lat_t.at[3, :, cut(k)], f_send.at[k], f_recv.at[k], (dp, sibling))
        for k in range(CHUNKS)
    ]
    near = remote(lat_t.at[0], lat_t.at[1], sib_sem.at[0], sib_sem.at[1], (dp, sibling))
    for c in over:
        c.start()
    near.start()

    def scatter(s, d):
        to = peer(d)
        return remote(
            part.at[s, pl.ds(pl.multiple_of(to * TILE, TILE), TILE)], rs_buf.at[s, d],
            rs_send.at[s, d], rs_recv.at[s, d], (to, head),
        )

    def gather(s, d):
        row = pl.multiple_of(source[s] * lat_cols + dp * TILE, TILE)
        block = grad.at[pl.ds(row, TILE)]
        return remote(block, block, ag_send.at[s, d], ag_recv.at[s, d], (peer(d), head))

    def finish(s, total):
        acc[s] = total
        part[s] = total.astype(jnp.bfloat16)
        for d in range(1, n_dp):
            scatter(s, d).start()

    def reduce(s):
        total = acc[s, pl.ds(pl.multiple_of(dp * TILE, TILE), TILE), :]
        for d in range(1, n_dp):
            scatter(s, d).wait_recv()
            total = total + rs_buf[s, d].astype(jnp.float32)
        row = pl.multiple_of(source[s] * lat_cols + dp * TILE, TILE)
        grad[pl.ds(row, TILE), :] = total.astype(jnp.bfloat16)
        for d in range(1, n_dp):
            gather(s, d).start()

    def product(s, k=None):
        if k is None:
            return dot_f32(lat_t[s], vg_v[...], ((1,), (0,)))
        return dot_f32(lat_t[s, :, cut(k)], vg_v[cut(k), :], ((1,), (0,)))

    load_vg.wait()
    finish(0, product(0))
    near.wait_recv()
    finish(1, product(1))

    for k in range(CHUNKS):
        over[k].wait_recv()
        forward[k].start()
        acc[2] = product(2, k) if k == 0 else acc[2] + product(2, k)
        if k < 2:
            reduce(k)
    finish(2, acc[2])
    for k in range(CHUNKS):
        forward[k].wait_recv()
        acc[3] = product(3, k) if k == 0 else acc[3] + product(3, k)
    finish(3, acc[3])
    reduce(2)
    reduce(3)
    for s in range(4):
        for d in range(1, n_dp):
            gather(s, d).wait_recv()

    count = grad.shape[1] // V_DIM
    done = newton_schulz([grad[:, pl.ds(h * V_DIM, V_DIM)] for h in range(count)])
    for h in range(count):
        out_ref[h] = done[h]

    near.wait_send()
    for k in range(CHUNKS):
        over[k].wait_send()
        forward[k].wait_send()
    for s in range(4):
        for d in range(1, n_dp):
            scatter(s, d).wait_send()
            gather(s, d).wait_send()


def kernel_body(n_dp, latent, value_grad, lengths):
    capacity, lat_cols = latent.shape
    width = value_grad.shape[1]
    dma = pltpu.SemaphoreType.DMA
    return pl.pallas_call(
        functools.partial(kernel, n_dp),
        out_shape=jax.ShapeDtypeStruct((width // V_DIM, KV_RANK, V_DIM), jnp.bfloat16),
        in_specs=[
            pl.BlockSpec(memory_space=pltpu.SMEM),
            pl.BlockSpec(memory_space=pl.ANY),
            pl.BlockSpec(memory_space=pl.ANY),
        ],
        out_specs=pl.BlockSpec(memory_space=pltpu.VMEM),
        scratch_shapes=[
            pltpu.VMEM((capacity, lat_cols), jnp.bfloat16),
            pltpu.VMEM((capacity, width), jnp.bfloat16),
            pltpu.VMEM((4, lat_cols, capacity), jnp.bfloat16),
            pltpu.VMEM((4, lat_cols, width), jnp.float32),
            pltpu.VMEM((4, lat_cols, width), jnp.bfloat16),
            pltpu.VMEM((4, n_dp, TILE, width), jnp.bfloat16),
            pltpu.VMEM((KV_RANK, width), jnp.bfloat16),
            dma((2,)), dma((2,)),
            dma((CHUNKS,)), dma((CHUNKS,)), dma((CHUNKS,)), dma((CHUNKS,)),
            dma((4, n_dp)), dma((4, n_dp)), dma((4, n_dp)), dma((4, n_dp)),
        ],
        compiler_params=pltpu.CompilerParams(
            collective_id=0, has_side_effects=True, vmem_limit_bytes=40 * 2**20
        ),
        name="muon_update",
    )(lengths, latent, value_grad)


def solution(mesh):
    n_dp, n_head = mesh.shape["dp"], mesh.shape["head"]
    fits = n_head == 4 and (KV_RANK // n_head) == TILE * n_dp
    body = functools.partial(kernel_body, n_dp) if fits else plain_body
    return jax.shard_map(
        body,
        mesh=mesh,
        in_specs=(P("dp", "head"), P("dp", "head"), P()),
        out_specs=P("head", None, None),
        check_vma=False,
    )
```

```python
import functools

import jax
import jax.numpy as jnp
from jax import lax
from jax.experimental import pallas as pl
from jax.experimental.pallas import tpu as pltpu
from jax.sharding import PartitionSpec as P

KV_RANK = 512
V_DIM = 128
ITERS = 5
ROW_PARTS = 2
TOKEN_PARTS = 2

epsilon = 1e-07
coef_one = 3.4445
coef_two = -4.775
coef_three = 2.0315


def plain_body(latent, value_grad, lengths):
    capacity, lat_cols = latent.shape
    grad_width = value_grad.shape[1]
    head_count = grad_width // V_DIM
    my_index = lax.axis_index("dp")
    own_length = lengths[my_index]
    slot_live = jnp.arange(capacity, dtype=jnp.int32) < own_length
    rows_grad = jnp.where(slot_live[:, None], value_grad, jnp.zeros_like(value_grad))
    partial_sum = lax.dot_general(
        lax.all_gather(latent, "head", axis=1, tiled=True),
        rows_grad,
        (((0,), (0,)), ((), ())),
        preferred_element_type=jnp.float32,
    )
    dw_shard = lax.psum_scatter(partial_sum, "dp", scatter_dimension=0, tiled=True)
    shard_heads = dw_shard.reshape(dw_shard.shape[0], head_count, V_DIM)
    local_squares = jnp.sum(shard_heads * shard_heads, axis=(0, 2))
    square_total = lax.psum(local_squares, "dp")
    head_norm = jnp.sqrt(square_total)
    ortho_shard = (shard_heads / (head_norm[None, :, None] + epsilon)).astype(jnp.bfloat16)
    ortho = lax.all_gather(ortho_shard, "dp", axis=0, tiled=True)
    for step in range(ITERS):
        gram_mat = jnp.einsum(
            "rhv,rhw->hvw", ortho, ortho, preferred_element_type=jnp.float32
        ).astype(jnp.bfloat16)
        squared = jnp.einsum("hvu,huw->hvw", gram_mat, gram_mat, preferred_element_type=jnp.float32)
        poly_mat = (coef_two * gram_mat.astype(jnp.float32) + coef_three * squared).astype(
            jnp.bfloat16
        )
        product = jnp.einsum("rhv,hvw->rhw", ortho, poly_mat, preferred_element_type=jnp.float32)
        ortho = (coef_one * ortho.astype(jnp.float32) + product).astype(jnp.bfloat16)
    scale = 0.2 * max(KV_RANK, V_DIM) ** 0.5
    update = (scale * ortho.astype(jnp.float32)).astype(jnp.bfloat16)
    return jnp.transpose(update, (1, 0, 2))


def dot_f32(a, b, dims):
    return lax.dot_general(a, b, (dims, ((), ())), preferred_element_type=jnp.float32)


def newton_schulz(grads):
    final = 0.2 * max(KV_RANK, V_DIM) ** 0.5
    xs = list(grads)
    inv = []
    for g in xs:
        w = g.astype(jnp.float32)
        rows = jnp.sum(w * w, axis=0, keepdims=True)
        inv.append(1.0 / (jnp.sqrt(jnp.sum(rows, axis=1, keepdims=True)) + epsilon))
    for step in range(ITERS):
        grams = [dot_f32(x, x, ((0,), (0,))) for x in xs]
        if step == 0:
            grams = [a * s * s for a, s in zip(grams, inv)]
        grams = [a.astype(jnp.bfloat16) for a in grams]
        squares = [dot_f32(a, a, ((1,), (0,))) for a in grams]
        polys = [
            (coef_two * a.astype(jnp.float32) + coef_three * q).astype(jnp.bfloat16)
            for a, q in zip(grams, squares)
        ]
        prods = [dot_f32(x, b, ((1,), (0,))) for x, b in zip(xs, polys)]
        wide = [coef_one * x.astype(jnp.float32) + p for x, p in zip(xs, prods)]
        if step == 0:
            wide = [x * s for x, s in zip(wide, inv)]
        xs = [x.astype(jnp.bfloat16) for x in wide]
    return [(final * x.astype(jnp.float32)).astype(jnp.bfloat16) for x in xs]


def kernel(
    depth,
    len_hbm, lat_hbm, vg_hbm, out_ref,
    len_s, lat_v, vg_v, lat_t, acc, part, ybuf, zacc, zpart, zbuf, grad,
    load_sem, sib_sem, x_send, x_recv, f_send, f_recv,
    y_send, y_recv, z_send, z_recv, a_send, a_recv, b_send, b_recv,
):
    dp = lax.axis_index("dp")
    head = lax.axis_index("head")
    y, z = lax.rem(dp, 2), lax.div(dp, 2)
    core = lax.rem(head, 2)
    sibling = head + 1 - 2 * core
    partner = lax.rem(head + 2, 4)
    far = lax.rem(sibling + 2, 4)
    source = (head, sibling, partner, far)
    across = dp + 1 - 2 * y
    lat_cols, capacity = lat_t.shape[1], lat_t.shape[2]
    half = acc.shape[3]
    part_rows = lat_cols // ROW_PARTS
    span = capacity // TOKEN_PARTS

    def along(d):
        return lax.rem(z + d, depth) * 2 + y

    loads = [
        pltpu.make_async_copy(src, dst, load_sem.at[i])
        for i, (src, dst) in enumerate(((lat_hbm, lat_v), (len_hbm, len_s), (vg_hbm, vg_v)))
    ]
    for c in loads:
        c.start()

    barrier = pltpu.get_barrier_semaphore()
    friends = [(dp, sibling), (dp, partner), (across, head)]
    friends += [(along(d), head) for d in range(1, depth)]
    for where in friends:
        pl.semaphore_signal(barrier, inc=1, device_id=where, device_id_type=pl.DeviceIdType.MESH)

    loads[0].wait()
    loads[1].wait()
    live = lax.broadcasted_iota(jnp.int32, (lat_cols, capacity), 1) < len_s[dp]
    turned = lat_v[...].T
    lat_t[0] = jnp.where(live, turned, jnp.zeros_like(turned))
    pl.semaphore_wait(barrier, len(friends))

    def remote(src, dst, ssem, rsem, where):
        return pltpu.make_async_remote_copy(
            src_ref=src, dst_ref=dst, send_sem=ssem, recv_sem=rsem,
            device_id=where, device_id_type=pl.DeviceIdType.MESH,
        )

    pieces = [(c, k) for c in range(ROW_PARTS) for k in range(TOKEN_PARTS)]

    def piece(slot, i):
        c, k = pieces[i]
        return lat_t.at[slot, pl.ds(c * part_rows, part_rows), pl.ds(k * span, span)]

    over = [
        remote(piece(0, i), piece(2, i), x_send.at[i], x_recv.at[i], (dp, partner))
        for i in range(len(pieces))
    ]
    forward = [
        remote(piece(2, i), piece(3, i), f_send.at[i], f_recv.at[i], (dp, sibling))
        for i in range(len(pieces))
    ]
    near = remote(lat_t.at[0], lat_t.at[1], sib_sem.at[0], sib_sem.at[1], (dp, sibling))
    over[0].start()
    near.start()
    for c in over[1:]:
        c.start()

    units = [(0, 0, lat_cols), (1, 0, lat_cols)]
    units += [(s, c * part_rows, part_rows) for c in range(ROW_PARTS) for s in (2, 3)]

    def spot(u, zz):
        s, row, rows = units[u]
        block = rows // depth
        return pl.ds(pl.multiple_of(row + zz * block, block), block)

    def grad_rows(u, zz=None):
        s, row, rows = units[u]
        if zz is None:
            return pl.ds(pl.multiple_of(source[s] * lat_cols + row, rows), rows)
        block = rows // depth
        return pl.ds(pl.multiple_of(source[s] * lat_cols + row + zz * block, block), block)

    def swap(u):
        s, row, rows = units[u]
        return remote(
            part.at[s, 1 - y, pl.ds(row, rows)], ybuf.at[s, pl.ds(row, rows)],
            y_send.at[u], y_recv.at[u], (across, head),
        )

    def scatter(u, d):
        s, row, rows = units[u]
        return remote(
            zpart.at[s, spot(u, lax.rem(z + d, depth))],
            zbuf.at[s, d, pl.ds(row // depth, rows // depth)],
            z_send.at[u, d], z_recv.at[u, d], (along(d), head),
        )

    def gather(u, d):
        block = grad.at[y, grad_rows(u, z)]
        return remote(block, block, a_send.at[u, d], a_recv.at[u, d], (along(d), head))

    def share(u):
        block = grad.at[y, grad_rows(u)]
        return remote(block, block, b_send.at[u], b_recv.at[u], (across, head))

    def multiply(u, k=None):
        s, row, rows = units[u]
        tokens = pl.ds(0, capacity) if k is None else pl.ds(k * span, span)
        lhs = lat_t[s, pl.ds(row, rows), tokens]
        for j in range(2):
            value = dot_f32(lhs, vg_v[tokens, pl.ds(j * half, half)], ((1,), (0,)))
            if k:
                value = value + acc[s, j, pl.ds(row, rows), :]
            acc[s, j, pl.ds(row, rows), :] = value
            if k is None or k == TOKEN_PARTS - 1:
                part[s, j, pl.ds(row, rows), :] = value.astype(jnp.bfloat16)
        if k is None or k == TOKEN_PARTS - 1:
            swap(u).start()

    def stage_z(u):
        s, row, rows = units[u]
        here = pl.ds(row, rows)
        swap(u).wait_recv()
        total = acc[s, y, here, :] + ybuf[s, here, :].astype(jnp.float32)
        zacc[s, here, :] = total
        zpart[s, here, :] = total.astype(jnp.bfloat16)
        for d in range(1, depth):
            scatter(u, d).start()

    def stage_gather(u):
        s, row, rows = units[u]
        total = zacc[s, spot(u, z), :]
        for d in range(1, depth):
            scatter(u, d).wait_recv()
            total = total + zbuf[s, d, pl.ds(row // depth, rows // depth), :].astype(jnp.float32)
        grad[y, grad_rows(u, z), :] = total.astype(jnp.bfloat16)
        for d in range(1, depth):
            gather(u, d).start()

    def stage_share(u):
        for d in range(1, depth):
            gather(u, d).wait_recv()
        share(u).start()

    def arrive(i):
        over[i].wait_recv()
        forward[i].start()

    loads[2].wait()
    multiply(0)
    near.wait_recv()
    multiply(1)
    arrive(0)
    multiply(2, 0)
    stage_z(0)
    arrive(1)
    multiply(2, 1)
    stage_z(1)
    for i in (0, 1):
        forward[i].wait_recv()
        multiply(3, i)
    stage_gather(0)
    stage_gather(1)
    arrive(2)
    multiply(4, 0)
    stage_z(2)
    stage_share(0)
    arrive(3)
    multiply(4, 1)
    stage_z(3)
    for i in (2, 3):
        forward[i].wait_recv()
        multiply(5, i - 2)
    stage_share(1)
    stage_gather(2)
    stage_gather(3)
    stage_z(4)
    stage_z(5)
    stage_share(2)
    stage_share(3)
    stage_gather(4)
    stage_gather(5)
    stage_share(4)
    stage_share(5)

    count = half // V_DIM

    def orthogonalize(side):
        done = newton_schulz([grad[side, :, pl.ds(h * V_DIM, V_DIM)] for h in range(count)])
        for h in range(count):
            out_ref[side * count + h] = done[h]

    orthogonalize(y)
    for u in range(len(units)):
        share(u).wait_recv()
    orthogonalize(1 - y)

    near.wait_send()
    for i in range(len(pieces)):
        over[i].wait_send()
        forward[i].wait_send()
    for u in range(len(units)):
        swap(u).wait_send()
        share(u).wait_send()
        for d in range(1, depth):
            scatter(u, d).wait_send()
            gather(u, d).wait_send()


def kernel_body(depth, latent, value_grad, lengths):
    capacity, lat_cols = latent.shape
    width = value_grad.shape[1]
    half = width // 2
    units, pieces = 2 + 2 * ROW_PARTS, ROW_PARTS * TOKEN_PARTS
    dma = pltpu.SemaphoreType.DMA
    low, full = jnp.bfloat16, jnp.float32
    return pl.pallas_call(
        functools.partial(kernel, depth),
        out_shape=jax.ShapeDtypeStruct((width // V_DIM, KV_RANK, V_DIM), low),
        in_specs=[pl.BlockSpec(memory_space=pltpu.HBM)] * 3,
        out_specs=pl.BlockSpec(memory_space=pltpu.VMEM),
        scratch_shapes=[
            pltpu.SMEM(lengths.shape, jnp.int32),
            pltpu.VMEM((capacity, lat_cols), low),
            pltpu.VMEM((capacity, width), low),
            pltpu.VMEM((4, lat_cols, capacity), low),
            pltpu.VMEM((4, 2, lat_cols, half), full),
            pltpu.VMEM((4, 2, lat_cols, half), low),
            pltpu.VMEM((4, lat_cols, half), low),
            pltpu.VMEM((4, lat_cols, half), full),
            pltpu.VMEM((4, lat_cols, half), low),
            pltpu.VMEM((4, depth, lat_cols // depth, half), low),
            pltpu.VMEM((2, KV_RANK, half), low),
            dma((3,)), dma((2,)),
            dma((pieces,)), dma((pieces,)), dma((pieces,)), dma((pieces,)),
            dma((units,)), dma((units,)),
            dma((units, depth)), dma((units, depth)),
            dma((units, depth)), dma((units, depth)),
            dma((units,)), dma((units,)),
        ],
        compiler_params=pltpu.CompilerParams(
            collective_id=0, has_side_effects=True, vmem_limit_bytes=48 * 2**20
        ),
        name="muon_update",
    )(lengths, latent, value_grad)


def solution(mesh):
    n_dp, n_head = mesh.shape["dp"], mesh.shape["head"]
    depth = n_dp // 2
    fits = n_head == 4 and KV_RANK // n_head == 16 * ROW_PARTS * depth
    body = functools.partial(kernel_body, depth) if fits else plain_body
    return jax.shard_map(
        body,
        mesh=mesh,
        in_specs=(P("dp", "head"), P("dp", "head"), P()),
        out_specs=P("head", None, None),
        check_vma=False,
    )
```

```python
import functools

import jax
import jax.numpy as jnp
from jax import lax
from jax.experimental import pallas as pl
from jax.experimental.pallas import tpu as pltpu
from jax.sharding import PartitionSpec as P

KV_RANK = 512
V_DIM = 128
ITERS = 5
ROW_PARTS = 2
TOKEN_PARTS = 2

epsilon = 1e-07
coef_one = 3.4445
coef_two = -4.775
coef_three = 2.0315


def plain_body(latent, value_grad, lengths):
    capacity, lat_cols = latent.shape
    grad_width = value_grad.shape[1]
    head_count = grad_width // V_DIM
    my_index = lax.axis_index("dp")
    own_length = lengths[my_index]
    slot_live = jnp.arange(capacity, dtype=jnp.int32) < own_length
    rows_grad = jnp.where(slot_live[:, None], value_grad, jnp.zeros_like(value_grad))
    partial_sum = lax.dot_general(
        lax.all_gather(latent, "head", axis=1, tiled=True),
        rows_grad,
        (((0,), (0,)), ((), ())),
        preferred_element_type=jnp.float32,
    )
    dw_shard = lax.psum_scatter(partial_sum, "dp", scatter_dimension=0, tiled=True)
    shard_heads = dw_shard.reshape(dw_shard.shape[0], head_count, V_DIM)
    local_squares = jnp.sum(shard_heads * shard_heads, axis=(0, 2))
    square_total = lax.psum(local_squares, "dp")
    head_norm = jnp.sqrt(square_total)
    ortho_shard = (shard_heads / (head_norm[None, :, None] + epsilon)).astype(jnp.bfloat16)
    ortho = lax.all_gather(ortho_shard, "dp", axis=0, tiled=True)
    for step in range(ITERS):
        gram_mat = jnp.einsum(
            "rhv,rhw->hvw", ortho, ortho, preferred_element_type=jnp.float32
        ).astype(jnp.bfloat16)
        squared = jnp.einsum("hvu,huw->hvw", gram_mat, gram_mat, preferred_element_type=jnp.float32)
        poly_mat = (coef_two * gram_mat.astype(jnp.float32) + coef_three * squared).astype(
            jnp.bfloat16
        )
        product = jnp.einsum("rhv,hvw->rhw", ortho, poly_mat, preferred_element_type=jnp.float32)
        ortho = (coef_one * ortho.astype(jnp.float32) + product).astype(jnp.bfloat16)
    scale = 0.2 * max(KV_RANK, V_DIM) ** 0.5
    update = (scale * ortho.astype(jnp.float32)).astype(jnp.bfloat16)
    return jnp.transpose(update, (1, 0, 2))


def dot_f32(a, b, dims):
    return lax.dot_general(a, b, (dims, ((), ())), preferred_element_type=jnp.float32)


def newton_schulz(turned):
    final = 0.2 * max(KV_RANK, V_DIM) ** 0.5
    xs = list(turned)
    inv = []
    for g in xs:
        w = g.astype(jnp.float32)
        rows = jnp.sum(w * w, axis=0, keepdims=True)
        inv.append(1.0 / (jnp.sqrt(jnp.sum(rows, axis=1, keepdims=True)) + epsilon))
    for step in range(ITERS):
        grams = [dot_f32(x, x, ((1,), (1,))) for x in xs]
        if step == 0:
            grams = [a * s * s for a, s in zip(grams, inv)]
        grams = [a.astype(jnp.bfloat16) for a in grams]
        squares = [dot_f32(a, a, ((1,), (0,))) for a in grams]
        polys = [
            (coef_two * a.astype(jnp.float32) + coef_three * q).astype(jnp.bfloat16)
            for a, q in zip(grams, squares)
        ]
        prods = [dot_f32(b, x, ((1,), (0,))) for x, b in zip(xs, polys)]
        wide = [coef_one * x.astype(jnp.float32) + p for x, p in zip(xs, prods)]
        if step == 0:
            wide = [x * s for x, s in zip(wide, inv)]
        xs = [x.astype(jnp.bfloat16) for x in wide]
    return [(final * x.astype(jnp.float32)).astype(jnp.bfloat16).T for x in xs]


def kernel(
    depth,
    len_hbm, lat_hbm, vg_hbm, out_hbm,
    len_s, lat_v, vg_v, lat_t, acc, part, ybuf, zacc, zpart, zbuf, grad, out_v,
    load_sem, out_sem, sib_sem, x_send, x_recv, f_send, f_recv,
    y_send, y_recv, z_send, z_recv, a_send, a_recv, b_send, b_recv,
):
    dp = lax.axis_index("dp")
    head = lax.axis_index("head")
    y, z = lax.rem(dp, 2), lax.div(dp, 2)
    core = lax.rem(head, 2)
    sibling = head + 1 - 2 * core
    partner = lax.rem(head + 2, 4)
    far = lax.rem(sibling + 2, 4)
    source = (head, sibling, partner, far)
    across = dp + 1 - 2 * y
    lat_cols, capacity = lat_t.shape[1], lat_t.shape[2]
    half = acc.shape[3]
    part_rows = lat_cols // ROW_PARTS
    span = capacity // TOKEN_PARTS

    def along(d):
        return lax.rem(z + d, depth) * 2 + y

    loads = [
        pltpu.make_async_copy(src, dst, load_sem.at[i])
        for i, (src, dst) in enumerate(((lat_hbm, lat_v), (len_hbm, len_s), (vg_hbm, vg_v)))
    ]
    for c in loads:
        c.start()

    barrier = pltpu.get_barrier_semaphore()
    friends = [(dp, sibling), (dp, partner), (across, head)]
    friends += [(along(d), head) for d in range(1, depth)]
    for where in friends:
        pl.semaphore_signal(barrier, inc=1, device_id=where, device_id_type=pl.DeviceIdType.MESH)

    loads[0].wait()
    loads[1].wait()

    def turn(k):
        tokens = pl.ds(k * span, span)
        turned = lat_v[tokens, :].T
        live = lax.broadcasted_iota(jnp.int32, turned.shape, 1) + k * span < len_s[dp]
        lat_t[0, :, tokens] = jnp.where(live, turned, jnp.zeros_like(turned))

    turn(0)
    pl.semaphore_wait(barrier, len(friends))

    def remote(src, dst, ssem, rsem, where):
        return pltpu.make_async_remote_copy(
            src_ref=src, dst_ref=dst, send_sem=ssem, recv_sem=rsem,
            device_id=where, device_id_type=pl.DeviceIdType.MESH,
        )

    pieces = [(c, k) for c in range(ROW_PARTS) for k in range(TOKEN_PARTS)]

    def piece(slot, i):
        c, k = pieces[i]
        return lat_t.at[slot, pl.ds(c * part_rows, part_rows), pl.ds(k * span, span)]

    over = [
        remote(piece(0, i), piece(2, i), x_send.at[i], x_recv.at[i], (dp, partner))
        for i in range(len(pieces))
    ]
    forward = [
        remote(piece(2, i), piece(3, i), f_send.at[i], f_recv.at[i], (dp, sibling))
        for i in range(len(pieces))
    ]
    near = remote(lat_t.at[0], lat_t.at[1], sib_sem.at[0], sib_sem.at[1], (dp, sibling))
    over[0].start()
    for k in range(1, TOKEN_PARTS):
        turn(k)
    near.start()
    for c in over[1:]:
        c.start()

    units = [(0, 0, lat_cols)]
    units += [(2, c * part_rows, part_rows) for c in range(ROW_PARTS)]

    def rows_of(u):
        s, row, rows = units[u]
        return pl.ds(s, 2), pl.ds(row, rows)

    def block_of(u, zz):
        s, row, rows = units[u]
        block = rows // depth
        return pl.ds(s, 2), pl.ds(pl.multiple_of(row + zz * block, block), block)

    def buffer_of(u):
        s, row, rows = units[u]
        return pl.ds(s, 2), pl.ds(row // depth, rows // depth)

    def swap(u):
        slots, here = rows_of(u)
        return remote(
            part.at[1 - y, slots, here], ybuf.at[slots, here],
            y_send.at[u], y_recv.at[u], (across, head),
        )

    def scatter(u, d):
        return remote(
            zpart.at[block_of(u, lax.rem(z + d, depth))], zbuf.at[(d,) + buffer_of(u)],
            z_send.at[u, d], z_recv.at[u, d], (along(d), head),
        )

    def gather(u, d):
        block = grad.at[(y,) + block_of(u, z)]
        return remote(block, block, a_send.at[u, d], a_recv.at[u, d], (along(d), head))

    def share(u):
        block = grad.at[(y,) + rows_of(u)]
        return remote(block, block, b_send.at[u], b_recv.at[u], (across, head))

    def multiply(s, row, rows, k=None):
        tokens = pl.ds(0, capacity) if k is None else pl.ds(k * span, span)
        here = pl.ds(row, rows)
        lhs = lat_t[s, here, tokens]
        for j in range(2):
            value = dot_f32(lhs, vg_v[tokens, pl.ds(j * half, half)], ((1,), (0,)))
            if k:
                value = value + acc[j, s, here, :]
            acc[j, s, here, :] = value
            if k is None or k == TOKEN_PARTS - 1:
                part[j, s, here, :] = value.astype(jnp.bfloat16)

    def stage_z(u):
        here = rows_of(u)
        swap(u).wait_recv()
        total = acc[(y,) + here] + ybuf[here].astype(jnp.float32)
        zacc[here] = total
        zpart[here] = total.astype(jnp.bfloat16)
        for d in range(1, depth):
            scatter(u, d).start()

    def stage_gather(u):
        total = zacc[block_of(u, z)]
        for d in range(1, depth):
            scatter(u, d).wait_recv()
            total = total + zbuf[(d,) + buffer_of(u)].astype(jnp.float32)
        grad[(y,) + block_of(u, z)] = total.astype(jnp.bfloat16)
        for d in range(1, depth):
            gather(u, d).start()

    def stage_share(u):
        for d in range(1, depth):
            gather(u, d).wait_recv()
        share(u).start()

    def arrive(i):
        over[i].wait_recv()
        forward[i].start()

    loads[2].wait()
    multiply(0, 0, lat_cols)
    near.wait_recv()
    multiply(1, 0, lat_cols)
    swap(0).start()
    for c in range(ROW_PARTS):
        first = c * TOKEN_PARTS
        for k in range(TOKEN_PARTS):
            arrive(first + k)
            multiply(2, c * part_rows, part_rows, k)
            if c == 0 and k == 0:
                stage_z(0)
            if c == 1 and k == 0:
                stage_z(1)
        if c == 0:
            stage_gather(0)
        for k in range(TOKEN_PARTS):
            forward[first + k].wait_recv()
            multiply(3, c * part_rows, part_rows, k)
        swap(1 + c).start()
    stage_share(0)
    stage_gather(1)
    stage_z(2)
    stage_share(1)
    stage_gather(2)
    stage_share(2)

    count = half // V_DIM

    def orthogonalize(side):
        whole = grad[side].reshape(4 * lat_cols, half).T
        done = newton_schulz([whole[h * V_DIM : (h + 1) * V_DIM] for h in range(count)])
        for h in range(count):
            for s in range(4):
                row = pl.multiple_of(source[s] * lat_cols, lat_cols)
                out_v[side, h, pl.ds(row, lat_cols), :] = done[h][s * lat_cols : (s + 1) * lat_cols]

    def store(i, side):
        return pltpu.make_async_copy(
            out_v.at[side], out_hbm.at[pl.ds(side * count, count)], out_sem.at[i]
        )

    orthogonalize(y)
    store(0, y).start()
    for u in range(len(units)):
        share(u).wait_recv()
    orthogonalize(1 - y)
    store(1, 1 - y).start()

    near.wait_send()
    for i in range(len(pieces)):
        over[i].wait_send()
        forward[i].wait_send()
    for u in range(len(units)):
        swap(u).wait_send()
        share(u).wait_send()
        for d in range(1, depth):
            scatter(u, d).wait_send()
            gather(u, d).wait_send()
    store(0, y).wait()
    store(1, 1 - y).wait()


def kernel_body(depth, latent, value_grad, lengths):
    capacity, lat_cols = latent.shape
    width = value_grad.shape[1]
    half = width // 2
    units, pieces = 1 + ROW_PARTS, ROW_PARTS * TOKEN_PARTS
    dma = pltpu.SemaphoreType.DMA
    low, full = jnp.bfloat16, jnp.float32
    return pl.pallas_call(
        functools.partial(kernel, depth),
        out_shape=jax.ShapeDtypeStruct((width // V_DIM, KV_RANK, V_DIM), low),
        in_specs=[pl.BlockSpec(memory_space=pltpu.HBM)] * 3,
        out_specs=pl.BlockSpec(memory_space=pltpu.HBM),
        scratch_shapes=[
            pltpu.SMEM(lengths.shape, jnp.int32),
            pltpu.VMEM((capacity, lat_cols), low),
            pltpu.VMEM((capacity, width), low),
            pltpu.VMEM((4, lat_cols, capacity), low),
            pltpu.VMEM((2, 4, lat_cols, half), full),
            pltpu.VMEM((2, 4, lat_cols, half), low),
            pltpu.VMEM((4, lat_cols, half), low),
            pltpu.VMEM((4, lat_cols, half), full),
            pltpu.VMEM((4, lat_cols, half), low),
            pltpu.VMEM((depth, 4, lat_cols // depth, half), low),
            pltpu.VMEM((2, 4, lat_cols, half), low),
            pltpu.VMEM((2, half // V_DIM, KV_RANK, V_DIM), low),
            dma((3,)), dma((2,)), dma((2,)),
            dma((pieces,)), dma((pieces,)), dma((pieces,)), dma((pieces,)),
            dma((units,)), dma((units,)),
            dma((units, depth)), dma((units, depth)),
            dma((units, depth)), dma((units, depth)),
            dma((units,)), dma((units,)),
        ],
        compiler_params=pltpu.CompilerParams(
            collective_id=0, has_side_effects=True, vmem_limit_bytes=63 * 2**20
        ),
        name="muon_update",
    )(lengths, latent, value_grad)


def solution(mesh):
    n_dp, n_head = mesh.shape["dp"], mesh.shape["head"]
    depth = n_dp // 2
    fits = n_head == 4 and KV_RANK // n_head == 16 * ROW_PARTS * depth
    body = functools.partial(kernel_body, depth) if fits else plain_body
    return jax.shard_map(
        body,
        mesh=mesh,
        in_specs=(P("dp", "head"), P("dp", "head"), P()),
        out_specs=P("head", None, None),
        check_vma=False,
    )
```

```python
import functools

import jax
import jax.numpy as jnp
from jax import lax
from jax.experimental import pallas as pl
from jax.experimental.pallas import tpu as pltpu
from jax.sharding import PartitionSpec as P

KV_RANK = 512
V_DIM = 128
ITERS = 5
ROW_PARTS = 2
TOKEN_PARTS = 2

epsilon = 1e-07
coef_one = 3.4445
coef_two = -4.775
coef_three = 2.0315


def plain_body(latent, value_grad, lengths):
    capacity, lat_cols = latent.shape
    grad_width = value_grad.shape[1]
    head_count = grad_width // V_DIM
    my_index = lax.axis_index("dp")
    own_length = lengths[my_index]
    slot_live = jnp.arange(capacity, dtype=jnp.int32) < own_length
    rows_grad = jnp.where(slot_live[:, None], value_grad, jnp.zeros_like(value_grad))
    partial_sum = lax.dot_general(
        lax.all_gather(latent, "head", axis=1, tiled=True),
        rows_grad,
        (((0,), (0,)), ((), ())),
        preferred_element_type=jnp.float32,
    )
    dw_shard = lax.psum_scatter(partial_sum, "dp", scatter_dimension=0, tiled=True)
    shard_heads = dw_shard.reshape(dw_shard.shape[0], head_count, V_DIM)
    local_squares = jnp.sum(shard_heads * shard_heads, axis=(0, 2))
    square_total = lax.psum(local_squares, "dp")
    head_norm = jnp.sqrt(square_total)
    ortho_shard = (shard_heads / (head_norm[None, :, None] + epsilon)).astype(jnp.bfloat16)
    ortho = lax.all_gather(ortho_shard, "dp", axis=0, tiled=True)
    for step in range(ITERS):
        gram_mat = jnp.einsum(
            "rhv,rhw->hvw", ortho, ortho, preferred_element_type=jnp.float32
        ).astype(jnp.bfloat16)
        squared = jnp.einsum("hvu,huw->hvw", gram_mat, gram_mat, preferred_element_type=jnp.float32)
        poly_mat = (coef_two * gram_mat.astype(jnp.float32) + coef_three * squared).astype(
            jnp.bfloat16
        )
        product = jnp.einsum("rhv,hvw->rhw", ortho, poly_mat, preferred_element_type=jnp.float32)
        ortho = (coef_one * ortho.astype(jnp.float32) + product).astype(jnp.bfloat16)
    scale = 0.2 * max(KV_RANK, V_DIM) ** 0.5
    update = (scale * ortho.astype(jnp.float32)).astype(jnp.bfloat16)
    return jnp.transpose(update, (1, 0, 2))


def dot_f32(a, b, dims):
    return lax.dot_general(a, b, (dims, ((), ())), preferred_element_type=jnp.float32)


def newton_schulz(grads):
    wide = grads.astype(jnp.float32)
    inv = 1.0 / (jnp.sqrt(jnp.sum(wide * wide, axis=(1, 2), keepdims=True)) + epsilon)
    ortho = grads
    for step in range(ITERS):
        gram = jnp.einsum("hrv,hrw->hvw", ortho, ortho, preferred_element_type=jnp.float32)
        if step == 0:
            gram = gram * inv * inv
        gram = gram.astype(jnp.bfloat16)
        squared = jnp.einsum("hvu,huw->hvw", gram, gram, preferred_element_type=jnp.float32)
        poly = (coef_two * gram.astype(jnp.float32) + coef_three * squared).astype(jnp.bfloat16)
        product = jnp.einsum("hrv,hvw->hrw", ortho, poly, preferred_element_type=jnp.float32)
        wide = coef_one * ortho.astype(jnp.float32) + product
        if step == 0:
            wide = wide * inv
        ortho = wide.astype(jnp.bfloat16)
    scale = 0.2 * max(KV_RANK, V_DIM) ** 0.5
    return (scale * ortho.astype(jnp.float32)).astype(jnp.bfloat16)


def kernel(
    depth,
    len_hbm, lat_hbm, vg_hbm, grad,
    len_s, lat_v, vg_v, lat_t, acc, part, ybuf, zacc, zpart, zbuf,
    load_sem, sib_sem, x_send, x_recv, f_send, f_recv,
    y_send, y_recv, z_send, z_recv, a_send, a_recv, b_send, b_recv,
):
    dp = lax.axis_index("dp")
    head = lax.axis_index("head")
    y, z = lax.rem(dp, 2), lax.div(dp, 2)
    core = lax.rem(head, 2)
    sibling = head + 1 - 2 * core
    partner = lax.rem(head + 2, 4)
    far = lax.rem(sibling + 2, 4)
    source = (head, sibling, partner, far)
    across = dp + 1 - 2 * y
    lat_cols, capacity = lat_t.shape[1], lat_t.shape[2]
    half = acc.shape[3]
    count = half // V_DIM
    part_rows = lat_cols // ROW_PARTS
    span = capacity // TOKEN_PARTS

    def along(d):
        return lax.rem(z + d, depth) * 2 + y

    loads = [
        pltpu.make_async_copy(src, dst, load_sem.at[i])
        for i, (src, dst) in enumerate(((lat_hbm, lat_v), (len_hbm, len_s), (vg_hbm, vg_v)))
    ]
    for c in loads:
        c.start()

    barrier = pltpu.get_barrier_semaphore()
    friends = [(dp, sibling), (dp, partner), (across, head)]
    friends += [(along(d), head) for d in range(1, depth)]
    for where in friends:
        pl.semaphore_signal(barrier, inc=1, device_id=where, device_id_type=pl.DeviceIdType.MESH)

    loads[0].wait()
    loads[1].wait()

    def turn(k):
        tokens = pl.ds(k * span, span)
        turned = lat_v[tokens, :].T
        live = lax.broadcasted_iota(jnp.int32, turned.shape, 1) + k * span < len_s[dp]
        lat_t[0, :, tokens] = jnp.where(live, turned, jnp.zeros_like(turned))

    turn(0)
    pl.semaphore_wait(barrier, len(friends))

    def remote(src, dst, ssem, rsem, where):
        return pltpu.make_async_remote_copy(
            src_ref=src, dst_ref=dst, send_sem=ssem, recv_sem=rsem,
            device_id=where, device_id_type=pl.DeviceIdType.MESH,
        )

    pieces = [(c, k) for c in range(ROW_PARTS) for k in range(TOKEN_PARTS)]

    def piece(slot, i):
        c, k = pieces[i]
        return lat_t.at[slot, pl.ds(c * part_rows, part_rows), pl.ds(k * span, span)]

    over = [
        remote(piece(0, i), piece(2, i), x_send.at[i], x_recv.at[i], (dp, partner))
        for i in range(len(pieces))
    ]
    forward = [
        remote(piece(2, i), piece(3, i), f_send.at[i], f_recv.at[i], (dp, sibling))
        for i in range(len(pieces))
    ]
    near = remote(lat_t.at[0], lat_t.at[1], sib_sem.at[0], sib_sem.at[1], (dp, sibling))
    over[0].start()
    for k in range(1, TOKEN_PARTS):
        turn(k)
    near.start()
    for c in over[1:]:
        c.start()

    own, other = head - core, partner - core
    units = [(own, 0, lat_cols)]
    units += [(other, c * part_rows, part_rows) for c in range(ROW_PARTS)]

    def rows_of(u):
        s, row, rows = units[u]
        return pl.ds(s, 2), pl.ds(row, rows)

    def block_of(u, zz):
        s, row, rows = units[u]
        block = rows // depth
        return pl.ds(s, 2), pl.ds(pl.multiple_of(row + zz * block, block), block)

    def buffer_of(u):
        s, row, rows = units[u]
        return pl.ds(s, 2), pl.ds(row // depth, rows // depth)

    def swap(u):
        slots, here = rows_of(u)
        return remote(
            part.at[1 - y, slots, here], ybuf.at[slots, here],
            y_send.at[u], y_recv.at[u], (across, head),
        )

    def scatter(u, d):
        return remote(
            zpart.at[block_of(u, lax.rem(z + d, depth))], zbuf.at[(d,) + buffer_of(u)],
            z_send.at[u, d], z_recv.at[u, d], (along(d), head),
        )

    def gather(u, d):
        block = grad.at[(pl.ds(y * count, count),) + block_of(u, z)]
        return remote(block, block, a_send.at[u, d], a_recv.at[u, d], (along(d), head))

    def share(u):
        block = grad.at[(pl.ds(y * count, count),) + rows_of(u)]
        return remote(block, block, b_send.at[u], b_recv.at[u], (across, head))

    def multiply(s, row, rows, k=None):
        tokens = pl.ds(0, capacity) if k is None else pl.ds(k * span, span)
        here = pl.ds(row, rows)
        lhs = lat_t[s, here, tokens]
        for j in range(2):
            value = dot_f32(lhs, vg_v[tokens, pl.ds(j * half, half)], ((1,), (0,)))
            if k:
                value = value + acc[j, source[s], here, :]
            acc[j, source[s], here, :] = value
            if k is None or k == TOKEN_PARTS - 1:
                part[j, source[s], here, :] = value.astype(jnp.bfloat16)

    def stage_z(u):
        here = rows_of(u)
        swap(u).wait_recv()
        total = acc[(y,) + here] + ybuf[here].astype(jnp.float32)
        zacc[here] = total
        zpart[here] = total.astype(jnp.bfloat16)
        for d in range(1, depth):
            scatter(u, d).start()

    def stage_gather(u):
        total = zacc[block_of(u, z)]
        for d in range(1, depth):
            scatter(u, d).wait_recv()
            total = total + zbuf[(d,) + buffer_of(u)].astype(jnp.float32)
        for h in range(count):
            columns = total[..., h * V_DIM : (h + 1) * V_DIM]
            grad[(y * count + h,) + block_of(u, z)] = columns.astype(jnp.bfloat16)
        for d in range(1, depth):
            gather(u, d).start()

    def stage_share(u):
        for d in range(1, depth):
            gather(u, d).wait_recv()
        share(u).start()

    def arrive(i):
        over[i].wait_recv()
        forward[i].start()

    loads[2].wait()
    multiply(0, 0, lat_cols)
    near.wait_recv()
    multiply(1, 0, lat_cols)
    swap(0).start()
    for c in range(ROW_PARTS):
        first = c * TOKEN_PARTS
        for k in range(TOKEN_PARTS):
            arrive(first + k)
            multiply(2, c * part_rows, part_rows, k)
            if c == 0 and k == 0:
                stage_z(0)
            if c == 1 and k == 0:
                stage_z(1)
        if c == 0:
            stage_gather(0)
        for k in range(TOKEN_PARTS):
            forward[first + k].wait_recv()
            multiply(3, c * part_rows, part_rows, k)
        swap(1 + c).start()
    stage_share(0)
    stage_gather(1)
    stage_z(2)
    stage_share(1)
    stage_gather(2)
    stage_share(2)

    for u in range(len(units)):
        share(u).wait_recv()

    near.wait_send()
    for i in range(len(pieces)):
        over[i].wait_send()
        forward[i].wait_send()
    for u in range(len(units)):
        swap(u).wait_send()
        share(u).wait_send()
        for d in range(1, depth):
            scatter(u, d).wait_send()
            gather(u, d).wait_send()


def kernel_body(depth, latent, value_grad, lengths):
    capacity, lat_cols = latent.shape
    width = value_grad.shape[1]
    half = width // 2
    units, pieces = 1 + ROW_PARTS, ROW_PARTS * TOKEN_PARTS
    dma = pltpu.SemaphoreType.DMA
    low, full = jnp.bfloat16, jnp.float32
    latent, value_grad, lengths = (
        pltpu.with_memory_space_constraint(a, pltpu.HBM) for a in (latent, value_grad, lengths)
    )
    sums = pl.pallas_call(
        functools.partial(kernel, depth),
        out_shape=pltpu.VMEM((width // V_DIM, 4, lat_cols, V_DIM), low),
        in_specs=[pl.BlockSpec(memory_space=pltpu.HBM)] * 3,
        out_specs=pl.BlockSpec(memory_space=pltpu.VMEM),
        scratch_shapes=[
            pltpu.SMEM(lengths.shape, jnp.int32),
            pltpu.VMEM((capacity, lat_cols), low),
            pltpu.VMEM((capacity, width), low),
            pltpu.VMEM((4, lat_cols, capacity), low),
            pltpu.VMEM((2, 4, lat_cols, half), full),
            pltpu.VMEM((2, 4, lat_cols, half), low),
            pltpu.VMEM((4, lat_cols, half), low),
            pltpu.VMEM((4, lat_cols, half), full),
            pltpu.VMEM((4, lat_cols, half), low),
            pltpu.VMEM((depth, 4, lat_cols // depth, half), low),
            dma((3,)), dma((2,)),
            dma((pieces,)), dma((pieces,)), dma((pieces,)), dma((pieces,)),
            dma((units,)), dma((units,)),
            dma((units, depth)), dma((units, depth)),
            dma((units, depth)), dma((units, depth)),
            dma((units,)), dma((units,)),
        ],
        compiler_params=pltpu.CompilerParams(
            collective_id=0, has_side_effects=True, vmem_limit_bytes=48 * 2**20
        ),
        name="gradient_sums",
    )(lengths, latent, value_grad)
    return newton_schulz(sums.reshape(width // V_DIM, KV_RANK, V_DIM))


def solution(mesh):
    n_dp, n_head = mesh.shape["dp"], mesh.shape["head"]
    depth = n_dp // 2
    fits = n_head == 4 and KV_RANK // n_head == 16 * ROW_PARTS * depth
    body = functools.partial(kernel_body, depth) if fits else plain_body
    return jax.shard_map(
        body,
        mesh=mesh,
        in_specs=(P("dp", "head"), P("dp", "head"), P()),
        out_specs=P("head", None, None),
        check_vma=False,
    )
```

```python
import functools

import jax
import jax.numpy as jnp
from jax import lax
from jax.experimental import pallas as pl
from jax.experimental.pallas import tpu as pltpu
from jax.sharding import PartitionSpec as P

KV_RANK = 512
V_DIM = 128
ITERS = 5
ROW_PARTS = 2
TOKEN_PARTS = 3

epsilon = 1e-07
coef_one = 3.4445
coef_two = -4.775
coef_three = 2.0315


def plain_body(latent, value_grad, lengths):
    capacity, lat_cols = latent.shape
    grad_width = value_grad.shape[1]
    head_count = grad_width // V_DIM
    my_index = lax.axis_index("dp")
    own_length = lengths[my_index]
    slot_live = jnp.arange(capacity, dtype=jnp.int32) < own_length
    rows_grad = jnp.where(slot_live[:, None], value_grad, jnp.zeros_like(value_grad))
    partial_sum = lax.dot_general(
        lax.all_gather(latent, "head", axis=1, tiled=True),
        rows_grad,
        (((0,), (0,)), ((), ())),
        preferred_element_type=jnp.float32,
    )
    dw_shard = lax.psum_scatter(partial_sum, "dp", scatter_dimension=0, tiled=True)
    shard_heads = dw_shard.reshape(dw_shard.shape[0], head_count, V_DIM)
    local_squares = jnp.sum(shard_heads * shard_heads, axis=(0, 2))
    square_total = lax.psum(local_squares, "dp")
    head_norm = jnp.sqrt(square_total)
    ortho_shard = (shard_heads / (head_norm[None, :, None] + epsilon)).astype(jnp.bfloat16)
    ortho = lax.all_gather(ortho_shard, "dp", axis=0, tiled=True)
    for step in range(ITERS):
        gram_mat = jnp.einsum(
            "rhv,rhw->hvw", ortho, ortho, preferred_element_type=jnp.float32
        ).astype(jnp.bfloat16)
        squared = jnp.einsum("hvu,huw->hvw", gram_mat, gram_mat, preferred_element_type=jnp.float32)
        poly_mat = (coef_two * gram_mat.astype(jnp.float32) + coef_three * squared).astype(
            jnp.bfloat16
        )
        product = jnp.einsum("rhv,hvw->rhw", ortho, poly_mat, preferred_element_type=jnp.float32)
        ortho = (coef_one * ortho.astype(jnp.float32) + product).astype(jnp.bfloat16)
    scale = 0.2 * max(KV_RANK, V_DIM) ** 0.5
    update = (scale * ortho.astype(jnp.float32)).astype(jnp.bfloat16)
    return jnp.transpose(update, (1, 0, 2))


def dot_f32(a, b, dims):
    return lax.dot_general(a, b, (dims, ((), ())), preferred_element_type=jnp.float32)


def newton_schulz(grads):
    wide = grads.astype(jnp.float32)
    inv = 1.0 / (jnp.sqrt(jnp.sum(wide * wide, axis=(1, 2), keepdims=True)) + epsilon)
    ortho = grads
    for step in range(ITERS):
        gram = jnp.einsum("hrv,hrw->hvw", ortho, ortho, preferred_element_type=jnp.float32)
        if step == 0:
            gram = gram * inv * inv
        gram = gram.astype(jnp.bfloat16)
        squared = jnp.einsum("hvu,huw->hvw", gram, gram, preferred_element_type=jnp.float32)
        poly = (coef_two * gram.astype(jnp.float32) + coef_three * squared).astype(jnp.bfloat16)
        product = jnp.einsum("hrv,hvw->hrw", ortho, poly, preferred_element_type=jnp.float32)
        wide = coef_one * ortho.astype(jnp.float32) + product
        if step == 0:
            wide = wide * inv
        ortho = wide.astype(jnp.bfloat16)
    scale = 0.2 * max(KV_RANK, V_DIM) ** 0.5
    return (scale * ortho.astype(jnp.float32)).astype(jnp.bfloat16)


def kernel(
    depth,
    len_hbm, lat_hbm, vg_hbm, grad,
    len_s, lat_v, vg_v, lat_t, acc, part, ybuf, zacc, zpart, zbuf, dbuf,
    load_sem, sib_sem, x_send, x_recv, f_send, f_recv,
    y_send, y_recv, z_send, z_recv, a_send, a_recv, b_send, b_recv,
    d_send, d_recv, e_send, e_recv,
):
    dp = lax.axis_index("dp")
    head = lax.axis_index("head")
    y, z = lax.rem(dp, 2), lax.div(dp, 2)
    core = lax.rem(head, 2)
    sibling = head + 1 - 2 * core
    partner = lax.rem(head + 2, 4)
    far = lax.rem(sibling + 2, 4)
    source = (head, sibling, partner, far)
    across = dp + 1 - 2 * y
    lat_cols, capacity = lat_t.shape[1], lat_t.shape[2]
    half = acc.shape[3]
    count = half // V_DIM
    part_rows = lat_cols // ROW_PARTS
    span = capacity // TOKEN_PARTS

    def along(d):
        return lax.rem(z + d, depth) * 2 + y

    def side(far_y):
        return 1 - y if far_y else y

    def other_dp(far_y, d):
        return lax.rem(z + d, depth) * 2 + side(far_y)

    loads = [
        pltpu.make_async_copy(src, dst, load_sem.at[i])
        for i, (src, dst) in enumerate(((lat_hbm, lat_v), (len_hbm, len_s), (vg_hbm, vg_v)))
    ]
    for c in loads:
        c.start()

    barrier = pltpu.get_barrier_semaphore()
    others = [(far_y, d) for far_y in range(2) for d in range(depth) if far_y or d]
    friends = [(dp, sibling), (dp, partner)]
    friends += [(other_dp(*o), head) for o in others]
    for where in friends:
        pl.semaphore_signal(barrier, inc=1, device_id=where, device_id_type=pl.DeviceIdType.MESH)

    loads[0].wait()
    loads[1].wait()

    def turn(k):
        tokens = pl.ds(k * span, span)
        turned = lat_v[tokens, :].T
        live = lax.broadcasted_iota(jnp.int32, turned.shape, 1) + k * span < len_s[dp]
        lat_t[0, :, tokens] = jnp.where(live, turned, jnp.zeros_like(turned))

    turn(0)
    pl.semaphore_wait(barrier, len(friends))

    def remote(src, dst, ssem, rsem, where):
        return pltpu.make_async_remote_copy(
            src_ref=src, dst_ref=dst, send_sem=ssem, recv_sem=rsem,
            device_id=where, device_id_type=pl.DeviceIdType.MESH,
        )

    pieces = [(c, k) for c in range(ROW_PARTS) for k in range(TOKEN_PARTS)]

    def piece(slot, i):
        c, k = pieces[i]
        return lat_t.at[slot, pl.ds(c * part_rows, part_rows), pl.ds(k * span, span)]

    over = [
        remote(piece(0, i), piece(2, i), x_send.at[i], x_recv.at[i], (dp, partner))
        for i in range(len(pieces))
    ]
    forward = [
        remote(piece(2, i), piece(3, i), f_send.at[i], f_recv.at[i], (dp, sibling))
        for i in range(len(pieces))
    ]
    near = remote(lat_t.at[0], lat_t.at[1], sib_sem.at[0], sib_sem.at[1], (dp, sibling))
    over[0].start()
    for k in range(1, TOKEN_PARTS):
        turn(k)
    near.start()
    for c in over[1:]:
        c.start()

    own, other = head - core, partner - core
    units = [(own, 0, lat_cols)]
    units += [(other, c * part_rows, part_rows) for c in range(ROW_PARTS)]

    def rows_of(u):
        s, row, rows = units[u]
        return pl.ds(s, 2), pl.ds(row, rows)

    def block_of(u, zz):
        s, row, rows = units[u]
        block = rows // depth
        return pl.ds(s, 2), pl.ds(pl.multiple_of(row + zz * block, block), block)

    def buffer_of(u):
        s, row, rows = units[u]
        return pl.ds(s, 2), pl.ds(row // depth, rows // depth)

    def swap(u):
        slots, here = rows_of(u)
        return remote(
            part.at[1 - y, slots, here], ybuf.at[slots, here],
            y_send.at[u], y_recv.at[u], (across, head),
        )

    def scatter(u, d):
        return remote(
            zpart.at[block_of(u, lax.rem(z + d, depth))], zbuf.at[(d,) + buffer_of(u)],
            z_send.at[u, d], z_recv.at[u, d], (along(d), head),
        )

    def gather(u, d):
        block = grad.at[(pl.ds(y * count, count),) + block_of(u, z)]
        return remote(block, block, a_send.at[u, d], a_recv.at[u, d], (along(d), head))

    def share(u):
        block = grad.at[(pl.ds(y * count, count),) + rows_of(u)]
        return remote(block, block, b_send.at[u], b_recv.at[u], (across, head))

    def scatter_all(u, far_y, d):
        i = far_y * depth + d
        return remote(
            part.at[(side(far_y),) + block_of(u, lax.rem(z + d, depth))], dbuf.at[i],
            d_send.at[i], d_recv.at[i], (other_dp(far_y, d), head),
        )

    def gather_all(u, far_y, d):
        i = far_y * depth + d
        block = grad.at[(pl.ds(y * count, count),) + block_of(u, z)]
        return remote(block, block, e_send.at[i], e_recv.at[i], (other_dp(far_y, d), head))

    def multiply(s, row, rows, k=None):
        tokens = pl.ds(0, capacity) if k is None else pl.ds(k * span, span)
        here = pl.ds(row, rows)
        lhs = jnp.concatenate([lat_t[i, here, tokens] for i in s], axis=0)
        for j in range(2):
            value = dot_f32(lhs, vg_v[tokens, pl.ds(j * half, half)], ((1,), (0,)))
            for n, i in enumerate(s):
                mine = value[n * rows : (n + 1) * rows]
                if k:
                    mine = mine + acc[j, source[i], here, :]
                acc[j, source[i], here, :] = mine
                if k is None or k == TOKEN_PARTS - 1:
                    part[j, source[i], here, :] = mine.astype(jnp.bfloat16)

    def stage_z(u):
        here = rows_of(u)
        swap(u).wait_recv()
        total = acc[(y,) + here] + ybuf[here].astype(jnp.float32)
        zacc[here] = total
        zpart[here] = total.astype(jnp.bfloat16)
        for d in range(1, depth):
            scatter(u, d).start()

    def stage_gather(u):
        total = zacc[block_of(u, z)]
        for d in range(1, depth):
            scatter(u, d).wait_recv()
            total = total + zbuf[(d,) + buffer_of(u)].astype(jnp.float32)
        keep(u, total)
        for d in range(1, depth):
            gather(u, d).start()

    def keep(u, total):
        for h in range(count):
            columns = total[..., h * V_DIM : (h + 1) * V_DIM]
            grad[(y * count + h,) + block_of(u, z)] = columns.astype(jnp.bfloat16)

    def reduce_all(u):
        total = acc[(y,) + block_of(u, z)]
        for o in others:
            scatter_all(u, *o).wait_recv()
            total = total + dbuf[o[0] * depth + o[1]].astype(jnp.float32)
        keep(u, total)
        for o in others:
            gather_all(u, *o).start()

    def stage_share(u):
        for d in range(1, depth):
            gather(u, d).wait_recv()
        share(u).start()

    def arrive(i):
        over[i].wait_recv()
        forward[i].start()

    last = len(units) - 1
    loads[2].wait()
    multiply([0], 0, lat_cols)
    near.wait_recv()
    multiply([1], 0, lat_cols)
    swap(0).start()
    for c in range(ROW_PARTS):
        for k in range(TOKEN_PARTS):
            i = c * TOKEN_PARTS + k
            arrive(i)
            if k == 1:
                stage_z(c)
            if c == 1 and k == 2:
                stage_gather(1)
            forward[i].wait_recv()
            multiply([2, 3], c * part_rows, part_rows, k)
        if c == 0:
            swap(1).start()
            stage_gather(0)
    for o in others:
        scatter_all(last, *o).start()
    stage_share(0)
    reduce_all(last)
    stage_share(1)
    for u in range(last):
        share(u).wait_recv()
    for o in others:
        gather_all(last, *o).wait_recv()

    near.wait_send()
    for i in range(len(pieces)):
        over[i].wait_send()
        forward[i].wait_send()
    for o in others:
        scatter_all(last, *o).wait_send()
        gather_all(last, *o).wait_send()
    for u in range(last):
        swap(u).wait_send()
        share(u).wait_send()
        for d in range(1, depth):
            scatter(u, d).wait_send()
            gather(u, d).wait_send()


def kernel_body(depth, latent, value_grad, lengths):
    capacity, lat_cols = latent.shape
    width = value_grad.shape[1]
    half = width // 2
    units, pieces = ROW_PARTS, ROW_PARTS * TOKEN_PARTS
    dma = pltpu.SemaphoreType.DMA
    low, full = jnp.bfloat16, jnp.float32
    latent, value_grad, lengths = (
        pltpu.with_memory_space_constraint(a, pltpu.HBM) for a in (latent, value_grad, lengths)
    )
    sums = pl.pallas_call(
        functools.partial(kernel, depth),
        out_shape=pltpu.VMEM((width // V_DIM, 4, lat_cols, V_DIM), low),
        in_specs=[pl.BlockSpec(memory_space=pltpu.HBM)] * 3,
        out_specs=pl.BlockSpec(memory_space=pltpu.VMEM),
        scratch_shapes=[
            pltpu.SMEM(lengths.shape, jnp.int32),
            pltpu.VMEM((capacity, lat_cols), low),
            pltpu.VMEM((capacity, width), low),
            pltpu.VMEM((4, lat_cols, capacity), low),
            pltpu.VMEM((2, 4, lat_cols, half), full),
            pltpu.VMEM((2, 4, lat_cols, half), low),
            pltpu.VMEM((4, lat_cols, half), low),
            pltpu.VMEM((4, lat_cols, half), full),
            pltpu.VMEM((4, lat_cols, half), low),
            pltpu.VMEM((depth, 4, lat_cols // depth, half), low),
            pltpu.VMEM((2 * depth, 2, lat_cols // ROW_PARTS // depth, half), low),
            dma((3,)), dma((2,)),
            dma((pieces,)), dma((pieces,)), dma((pieces,)), dma((pieces,)),
            dma((units,)), dma((units,)),
            dma((units, depth)), dma((units, depth)),
            dma((units, depth)), dma((units, depth)),
            dma((units,)), dma((units,)),
            dma((2 * depth,)), dma((2 * depth,)), dma((2 * depth,)), dma((2 * depth,)),
        ],
        compiler_params=pltpu.CompilerParams(
            collective_id=0, has_side_effects=True, vmem_limit_bytes=48 * 2**20
        ),
        name="gradient_sums",
    )(lengths, latent, value_grad)
    return newton_schulz(sums.reshape(width // V_DIM, KV_RANK, V_DIM))


def solution(mesh):
    n_dp, n_head = mesh.shape["dp"], mesh.shape["head"]
    depth = n_dp // 2
    fits = n_head == 4 and KV_RANK // n_head == 16 * ROW_PARTS * depth
    body = functools.partial(kernel_body, depth) if fits else plain_body
    return jax.shard_map(
        body,
        mesh=mesh,
        in_specs=(P("dp", "head"), P("dp", "head"), P()),
        out_specs=P("head", None, None),
        check_vma=False,
    )
```

```python
import functools

import jax
import jax.numpy as jnp
from jax import lax
from jax.experimental import pallas as pl
from jax.experimental.pallas import tpu as pltpu
from jax.sharding import PartitionSpec as P

KV_RANK = 512
V_DIM = 128
ITERS = 5
ROW_PARTS = 2
TOKEN_PARTS = 3

epsilon = 1e-07
coef_one = 3.4445
coef_two = -4.775
coef_three = 2.0315


def plain_body(latent, value_grad, lengths):
    capacity, lat_cols = latent.shape
    grad_width = value_grad.shape[1]
    head_count = grad_width // V_DIM
    my_index = lax.axis_index("dp")
    own_length = lengths[my_index]
    slot_live = jnp.arange(capacity, dtype=jnp.int32) < own_length
    rows_grad = jnp.where(slot_live[:, None], value_grad, jnp.zeros_like(value_grad))
    partial_sum = lax.dot_general(
        lax.all_gather(latent, "head", axis=1, tiled=True),
        rows_grad,
        (((0,), (0,)), ((), ())),
        preferred_element_type=jnp.float32,
    )
    dw_shard = lax.psum_scatter(partial_sum, "dp", scatter_dimension=0, tiled=True)
    shard_heads = dw_shard.reshape(dw_shard.shape[0], head_count, V_DIM)
    local_squares = jnp.sum(shard_heads * shard_heads, axis=(0, 2))
    square_total = lax.psum(local_squares, "dp")
    head_norm = jnp.sqrt(square_total)
    ortho_shard = (shard_heads / (head_norm[None, :, None] + epsilon)).astype(jnp.bfloat16)
    ortho = lax.all_gather(ortho_shard, "dp", axis=0, tiled=True)
    for step in range(ITERS):
        gram_mat = jnp.einsum(
            "rhv,rhw->hvw", ortho, ortho, preferred_element_type=jnp.float32
        ).astype(jnp.bfloat16)
        squared = jnp.einsum("hvu,huw->hvw", gram_mat, gram_mat, preferred_element_type=jnp.float32)
        poly_mat = (coef_two * gram_mat.astype(jnp.float32) + coef_three * squared).astype(
            jnp.bfloat16
        )
        product = jnp.einsum("rhv,hvw->rhw", ortho, poly_mat, preferred_element_type=jnp.float32)
        ortho = (coef_one * ortho.astype(jnp.float32) + product).astype(jnp.bfloat16)
    scale = 0.2 * max(KV_RANK, V_DIM) ** 0.5
    update = (scale * ortho.astype(jnp.float32)).astype(jnp.bfloat16)
    return jnp.transpose(update, (1, 0, 2))


def dot_f32(a, b, dims):
    return lax.dot_general(a, b, (dims, ((), ())), preferred_element_type=jnp.float32)


def newton_schulz(grads):
    wide = grads.astype(jnp.float32)
    inv = 1.0 / (jnp.sqrt(jnp.sum(wide * wide, axis=(1, 2), keepdims=True)) + epsilon)
    ortho = grads
    for step in range(ITERS):
        gram = jnp.einsum("hrv,hrw->hvw", ortho, ortho, preferred_element_type=jnp.float32)
        if step == 0:
            gram = gram * inv * inv
        gram = gram.astype(jnp.bfloat16)
        squared = jnp.einsum("hvu,huw->hvw", gram, gram, preferred_element_type=jnp.float32)
        poly = (coef_two * gram.astype(jnp.float32) + coef_three * squared).astype(jnp.bfloat16)
        product = jnp.einsum("hrv,hvw->hrw", ortho, poly, preferred_element_type=jnp.float32)
        wide = coef_one * ortho.astype(jnp.float32) + product
        if step == 0:
            wide = wide * inv
        ortho = wide.astype(jnp.bfloat16)
    scale = 0.2 * max(KV_RANK, V_DIM) ** 0.5
    return (scale * ortho.astype(jnp.float32)).astype(jnp.bfloat16)


def kernel(
    depth,
    len_hbm, lat_hbm, vg_hbm, grad,
    len_s, lat_v, vg_v, lat_t, acc, part, ybuf, zacc, zpart, zbuf, dbuf,
    load_sem, sib_sem, x_send, x_recv, f_send, f_recv,
    y_send, y_recv, z_send, z_recv, a_send, a_recv, b_send, b_recv,
    d_send, d_recv, e_send, e_recv,
):
    dp = lax.axis_index("dp")
    head = lax.axis_index("head")
    y, z = lax.rem(dp, 2), lax.div(dp, 2)
    core = lax.rem(head, 2)
    sibling = head + 1 - 2 * core
    partner = lax.rem(head + 2, 4)
    far = lax.rem(sibling + 2, 4)
    source = (head, sibling, partner, far)
    across = dp + 1 - 2 * y
    lat_cols, capacity = lat_t.shape[1], lat_t.shape[2]
    half = acc.shape[3]
    count = half // V_DIM
    part_rows = lat_cols // ROW_PARTS
    span = capacity // TOKEN_PARTS

    def along(d):
        return lax.rem(z + d, depth) * 2 + y

    def side(far_y):
        return 1 - y if far_y else y

    def other_dp(far_y, d):
        return lax.rem(z + d, depth) * 2 + side(far_y)

    loads = [
        pltpu.make_async_copy(src, dst, load_sem.at[i])
        for i, (src, dst) in enumerate(((lat_hbm, lat_v), (len_hbm, len_s), (vg_hbm, vg_v)))
    ]
    for c in loads:
        c.start()

    barrier = pltpu.get_barrier_semaphore()
    others = [(far_y, d) for far_y in range(2) for d in range(depth) if far_y or d]
    friends = [(dp, sibling), (dp, partner)]
    friends += [(other_dp(*o), head) for o in others]
    for where in friends:
        pl.semaphore_signal(barrier, inc=1, device_id=where, device_id_type=pl.DeviceIdType.MESH)

    loads[0].wait()
    loads[1].wait()

    def turn(k):
        tokens = pl.ds(k * span, span)
        turned = lat_v[tokens, :].T
        live = lax.broadcasted_iota(jnp.int32, turned.shape, 1) + k * span < len_s[dp]
        lat_t[0, :, tokens] = jnp.where(live, turned, jnp.zeros_like(turned))

    turn(0)
    pl.semaphore_wait(barrier, len(friends))

    def remote(src, dst, ssem, rsem, where):
        return pltpu.make_async_remote_copy(
            src_ref=src, dst_ref=dst, send_sem=ssem, recv_sem=rsem,
            device_id=where, device_id_type=pl.DeviceIdType.MESH,
        )

    pieces = [(c, k) for c in range(ROW_PARTS) for k in range(TOKEN_PARTS)]

    def piece(slot, i):
        c, k = pieces[i]
        return lat_t.at[slot, pl.ds(c * part_rows, part_rows), pl.ds(k * span, span)]

    over = [
        remote(piece(0, i), piece(2, i), x_send.at[i], x_recv.at[i], (dp, partner))
        for i in range(len(pieces))
    ]
    forward = [
        remote(piece(2, i), piece(3, i), f_send.at[i], f_recv.at[i], (dp, sibling))
        for i in range(len(pieces))
    ]
    near = remote(lat_t.at[0], lat_t.at[1], sib_sem.at[0], sib_sem.at[1], (dp, sibling))
    over[0].start()
    for k in range(1, TOKEN_PARTS):
        turn(k)
    near.start()
    for c in over[1:]:
        c.start()

    own, other = head - core, partner - core
    units = [(own, 0, lat_cols)]
    units += [(other, c * part_rows, part_rows) for c in range(ROW_PARTS)]

    def rows_of(u):
        s, row, rows = units[u]
        return pl.ds(s, 2), pl.ds(row, rows)

    def block_of(u, zz):
        s, row, rows = units[u]
        block = rows // depth
        return pl.ds(s, 2), pl.ds(pl.multiple_of(row + zz * block, block), block)

    def buffer_of(u):
        s, row, rows = units[u]
        return pl.ds(s, 2), pl.ds(row // depth, rows // depth)

    def swap(u):
        slots, here = rows_of(u)
        return remote(
            part.at[1 - y, slots, here], ybuf.at[slots, here],
            y_send.at[u], y_recv.at[u], (across, head),
        )

    def scatter(u, d):
        return remote(
            zpart.at[block_of(u, lax.rem(z + d, depth))], zbuf.at[(d,) + buffer_of(u)],
            z_send.at[u, d], z_recv.at[u, d], (along(d), head),
        )

    def gather(u, d):
        block = grad.at[(pl.ds(y * count, count),) + block_of(u, z)]
        return remote(block, block, a_send.at[u, d], a_recv.at[u, d], (along(d), head))

    def share(u):
        block = grad.at[(pl.ds(y * count, count),) + rows_of(u)]
        return remote(block, block, b_send.at[u], b_recv.at[u], (across, head))

    def scatter_all(u, far_y, d):
        i = far_y * depth + d
        return remote(
            part.at[(side(far_y),) + block_of(u, lax.rem(z + d, depth))], dbuf.at[i],
            d_send.at[i], d_recv.at[i], (other_dp(far_y, d), head),
        )

    def gather_all(u, far_y, d):
        i = far_y * depth + d
        block = grad.at[(pl.ds(y * count, count),) + block_of(u, z)]
        return remote(block, block, e_send.at[i], e_recv.at[i], (other_dp(far_y, d), head))

    def multiply(s, row, rows, k=None):
        tokens = pl.ds(0, capacity) if k is None else pl.ds(k * span, span)
        here = pl.ds(row, rows)
        lhs = jnp.concatenate([lat_t[i, here, tokens] for i in s], axis=0)
        for j in range(2):
            value = dot_f32(lhs, vg_v[tokens, pl.ds(j * half, half)], ((1,), (0,)))
            for n, i in enumerate(s):
                mine = value[n * rows : (n + 1) * rows]
                if k:
                    mine = mine + acc[j, source[i], here, :]
                acc[j, source[i], here, :] = mine
                if k is None or k == TOKEN_PARTS - 1:
                    part[j, source[i], here, :] = mine.astype(jnp.bfloat16)

    def stage_z(u):
        here = rows_of(u)
        swap(u).wait_recv()
        total = acc[(y,) + here] + ybuf[here].astype(jnp.float32)
        zacc[here] = total
        zpart[here] = total.astype(jnp.bfloat16)
        for d in range(1, depth):
            scatter(u, d).start()

    def stage_gather(u):
        total = zacc[block_of(u, z)]
        for d in range(1, depth):
            scatter(u, d).wait_recv()
            total = total + zbuf[(d,) + buffer_of(u)].astype(jnp.float32)
        keep(u, total)
        for d in range(1, depth):
            gather(u, d).start()

    def keep(u, total):
        for h in range(count):
            columns = total[..., h * V_DIM : (h + 1) * V_DIM]
            grad[(y * count + h,) + block_of(u, z)] = columns.astype(jnp.bfloat16)

    def reduce_all(u):
        total = acc[(y,) + block_of(u, z)]
        for o in others:
            scatter_all(u, *o).wait_recv()
            total = total + dbuf[o[0] * depth + o[1]].astype(jnp.float32)
        keep(u, total)
        for o in others:
            gather_all(u, *o).start()

    def stage_share(u):
        for d in range(1, depth):
            gather(u, d).wait_recv()
        share(u).start()

    def arrive(i):
        over[i].wait_recv()
        forward[i].start()

    last = len(units) - 1

    def multiply_piece(i):
        c, k = pieces[i]
        forward[i].wait_recv()
        multiply([2, 3], c * part_rows, part_rows, k)
        if i == TOKEN_PARTS - 1:
            swap(1).start()

    loads[2].wait()
    near.wait_recv()
    for k in range(TOKEN_PARTS):
        multiply([0, 1], 0, lat_cols, k)
        if k == 0:
            arrive(0)
    swap(0).start()
    for i in range(1, len(pieces)):
        arrive(i)
        multiply_piece(i - 1)
        if i == len(pieces) - 2:
            stage_z(0)
    stage_z(1)
    multiply_piece(len(pieces) - 1)
    for o in others:
        scatter_all(last, *o).start()
    stage_gather(0)
    stage_gather(1)
    reduce_all(last)
    stage_share(0)
    stage_share(1)
    for u in range(last):
        share(u).wait_recv()
    for o in others:
        gather_all(last, *o).wait_recv()

    near.wait_send()
    for i in range(len(pieces)):
        over[i].wait_send()
        forward[i].wait_send()
    for o in others:
        scatter_all(last, *o).wait_send()
        gather_all(last, *o).wait_send()
    for u in range(last):
        swap(u).wait_send()
        share(u).wait_send()
        for d in range(1, depth):
            scatter(u, d).wait_send()
            gather(u, d).wait_send()


def kernel_body(depth, latent, value_grad, lengths):
    capacity, lat_cols = latent.shape
    width = value_grad.shape[1]
    half = width // 2
    units, pieces = ROW_PARTS, ROW_PARTS * TOKEN_PARTS
    dma = pltpu.SemaphoreType.DMA
    low, full = jnp.bfloat16, jnp.float32
    latent, value_grad, lengths = (
        pltpu.with_memory_space_constraint(a, pltpu.HBM) for a in (latent, value_grad, lengths)
    )
    sums = pl.pallas_call(
        functools.partial(kernel, depth),
        out_shape=pltpu.VMEM((width // V_DIM, 4, lat_cols, V_DIM), low),
        in_specs=[pl.BlockSpec(memory_space=pltpu.HBM)] * 3,
        out_specs=pl.BlockSpec(memory_space=pltpu.VMEM),
        scratch_shapes=[
            pltpu.SMEM(lengths.shape, jnp.int32),
            pltpu.VMEM((capacity, lat_cols), low),
            pltpu.VMEM((capacity, width), low),
            pltpu.VMEM((4, lat_cols, capacity), low),
            pltpu.VMEM((2, 4, lat_cols, half), full),
            pltpu.VMEM((2, 4, lat_cols, half), low),
            pltpu.VMEM((4, lat_cols, half), low),
            pltpu.VMEM((4, lat_cols, half), full),
            pltpu.VMEM((4, lat_cols, half), low),
            pltpu.VMEM((depth, 4, lat_cols // depth, half), low),
            pltpu.VMEM((2 * depth, 2, lat_cols // ROW_PARTS // depth, half), low),
            dma((3,)), dma((2,)),
            dma((pieces,)), dma((pieces,)), dma((pieces,)), dma((pieces,)),
            dma((units,)), dma((units,)),
            dma((units, depth)), dma((units, depth)),
            dma((units, depth)), dma((units, depth)),
            dma((units,)), dma((units,)),
            dma((2 * depth,)), dma((2 * depth,)), dma((2 * depth,)), dma((2 * depth,)),
        ],
        compiler_params=pltpu.CompilerParams(
            collective_id=0, has_side_effects=True, vmem_limit_bytes=48 * 2**20
        ),
        name="gradient_sums",
    )(lengths, latent, value_grad)
    return newton_schulz(sums.reshape(width // V_DIM, KV_RANK, V_DIM))


def solution(mesh):
    n_dp, n_head = mesh.shape["dp"], mesh.shape["head"]
    depth = n_dp // 2
    fits = n_head == 4 and KV_RANK // n_head == 16 * ROW_PARTS * depth
    body = functools.partial(kernel_body, depth) if fits else plain_body
    return jax.shard_map(
        body,
        mesh=mesh,
        in_specs=(P("dp", "head"), P("dp", "head"), P()),
        out_specs=P("head", None, None),
        check_vma=False,
    )
```

```python
import functools

import jax
import jax.numpy as jnp
from jax import lax
from jax.experimental import pallas as pl
from jax.experimental.pallas import tpu as pltpu
from jax.sharding import PartitionSpec as P

KV_RANK = 512
V_DIM = 128
ITERS = 5
ROW_PARTS = 2
TOKEN_PARTS = 3

epsilon = 1e-07
coef_one = 3.4445
coef_two = -4.775
coef_three = 2.0315


def plain_body(latent, value_grad, lengths):
    capacity, lat_cols = latent.shape
    grad_width = value_grad.shape[1]
    head_count = grad_width // V_DIM
    my_index = lax.axis_index("dp")
    own_length = lengths[my_index]
    slot_live = jnp.arange(capacity, dtype=jnp.int32) < own_length
    rows_grad = jnp.where(slot_live[:, None], value_grad, jnp.zeros_like(value_grad))
    partial_sum = lax.dot_general(
        lax.all_gather(latent, "head", axis=1, tiled=True),
        rows_grad,
        (((0,), (0,)), ((), ())),
        preferred_element_type=jnp.float32,
    )
    dw_shard = lax.psum_scatter(partial_sum, "dp", scatter_dimension=0, tiled=True)
    shard_heads = dw_shard.reshape(dw_shard.shape[0], head_count, V_DIM)
    local_squares = jnp.sum(shard_heads * shard_heads, axis=(0, 2))
    square_total = lax.psum(local_squares, "dp")
    head_norm = jnp.sqrt(square_total)
    ortho_shard = (shard_heads / (head_norm[None, :, None] + epsilon)).astype(jnp.bfloat16)
    ortho = lax.all_gather(ortho_shard, "dp", axis=0, tiled=True)
    for step in range(ITERS):
        gram_mat = jnp.einsum(
            "rhv,rhw->hvw", ortho, ortho, preferred_element_type=jnp.float32
        ).astype(jnp.bfloat16)
        squared = jnp.einsum("hvu,huw->hvw", gram_mat, gram_mat, preferred_element_type=jnp.float32)
        poly_mat = (coef_two * gram_mat.astype(jnp.float32) + coef_three * squared).astype(
            jnp.bfloat16
        )
        product = jnp.einsum("rhv,hvw->rhw", ortho, poly_mat, preferred_element_type=jnp.float32)
        ortho = (coef_one * ortho.astype(jnp.float32) + product).astype(jnp.bfloat16)
    scale = 0.2 * max(KV_RANK, V_DIM) ** 0.5
    update = (scale * ortho.astype(jnp.float32)).astype(jnp.bfloat16)
    return jnp.transpose(update, (1, 0, 2))


def dot_f32(a, b, dims):
    return lax.dot_general(a, b, (dims, ((), ())), preferred_element_type=jnp.float32)


def newton_schulz(grads):
    wide = grads.astype(jnp.float32)
    inv = 1.0 / (jnp.sqrt(jnp.sum(wide * wide, axis=(1, 2), keepdims=True)) + epsilon)
    ortho = grads
    for step in range(ITERS):
        gram = jnp.einsum("hrv,hrw->hvw", ortho, ortho, preferred_element_type=jnp.float32)
        if step == 0:
            gram = gram * inv * inv
        gram = gram.astype(jnp.bfloat16)
        squared = jnp.einsum("hvu,huw->hvw", gram, gram, preferred_element_type=jnp.float32)
        poly = (coef_two * gram.astype(jnp.float32) + coef_three * squared).astype(jnp.bfloat16)
        product = jnp.einsum("hrv,hvw->hrw", ortho, poly, preferred_element_type=jnp.float32)
        wide = coef_one * ortho.astype(jnp.float32) + product
        if step == 0:
            wide = wide * inv
        ortho = wide.astype(jnp.bfloat16)
    scale = 0.2 * max(KV_RANK, V_DIM) ** 0.5
    return (scale * ortho.astype(jnp.float32)).astype(jnp.bfloat16)


def kernel(
    depth,
    len_hbm, lat_hbm, vg_hbm, grad,
    len_s, lat_v, vg_v, lat_t, acc, part, ybuf, zacc, zpart, zbuf, dbuf,
    load_sem, sib_sem, x_send, x_recv, f_send, f_recv,
    y_send, y_recv, z_send, z_recv, a_send, a_recv, b_send, b_recv,
    d_send, d_recv, e_send, e_recv,
):
    dp = lax.axis_index("dp")
    head = lax.axis_index("head")
    y, z = lax.rem(dp, 2), lax.div(dp, 2)
    core = lax.rem(head, 2)
    sibling = head + 1 - 2 * core
    partner = lax.rem(head + 2, 4)
    far = lax.rem(sibling + 2, 4)
    source = (head, sibling, partner, far)
    across = dp + 1 - 2 * y
    lat_cols, capacity = lat_t.shape[1], lat_t.shape[2]
    half = acc.shape[3]
    count = half // V_DIM
    part_rows = lat_cols // ROW_PARTS
    span = capacity // TOKEN_PARTS

    def along(d):
        return lax.rem(z + d, depth) * 2 + y

    def side(far_y):
        return 1 - y if far_y else y

    def other_dp(far_y, d):
        return lax.rem(z + d, depth) * 2 + side(far_y)

    loads = [
        pltpu.make_async_copy(src, dst, load_sem.at[i])
        for i, (src, dst) in enumerate(((lat_hbm, lat_v), (len_hbm, len_s), (vg_hbm, vg_v)))
    ]
    for c in loads:
        c.start()

    barrier = pltpu.get_barrier_semaphore()
    others = [(far_y, d) for far_y in range(2) for d in range(depth) if far_y or d]
    friends = [(dp, sibling), (dp, partner)]
    friends += [(other_dp(*o), head) for o in others]
    for where in friends:
        pl.semaphore_signal(barrier, inc=1, device_id=where, device_id_type=pl.DeviceIdType.MESH)

    loads[0].wait()
    loads[1].wait()

    def turn(k):
        tokens = pl.ds(k * span, span)
        turned = lat_v[tokens, :].T
        live = lax.broadcasted_iota(jnp.int32, turned.shape, 1) + k * span < len_s[dp]
        lat_t[0, :, tokens] = jnp.where(live, turned, jnp.zeros_like(turned))

    turn(0)
    pl.semaphore_wait(barrier, len(friends))

    def remote(src, dst, ssem, rsem, where):
        return pltpu.make_async_remote_copy(
            src_ref=src, dst_ref=dst, send_sem=ssem, recv_sem=rsem,
            device_id=where, device_id_type=pl.DeviceIdType.MESH,
        )

    pieces = [(c, k) for c in range(ROW_PARTS) for k in range(TOKEN_PARTS)]

    def piece(slot, i):
        c, k = pieces[i]
        return lat_t.at[slot, pl.ds(c * part_rows, part_rows), pl.ds(k * span, span)]

    over = [
        remote(piece(0, i), piece(2, i), x_send.at[i], x_recv.at[i], (dp, partner))
        for i in range(len(pieces))
    ]
    forward = [
        remote(piece(2, i), piece(3, i), f_send.at[i], f_recv.at[i], (dp, sibling))
        for i in range(len(pieces))
    ]
    near = remote(lat_t.at[0], lat_t.at[1], sib_sem.at[0], sib_sem.at[1], (dp, sibling))
    over[0].start()
    for k in range(1, TOKEN_PARTS):
        turn(k)
    near.start()
    for c in over[1:]:
        c.start()

    own, other = head - core, partner - core
    units = [(own, 0, lat_cols)]
    units += [(other, c * part_rows, part_rows) for c in range(ROW_PARTS)]

    def rows_of(u):
        s, row, rows = units[u]
        return pl.ds(s, 2), pl.ds(row, rows)

    def block_of(u, zz):
        s, row, rows = units[u]
        block = rows // depth
        return pl.ds(s, 2), pl.ds(pl.multiple_of(row + zz * block, block), block)

    def buffer_of(u):
        s, row, rows = units[u]
        return pl.ds(s, 2), pl.ds(row // depth, rows // depth)

    def swap(u):
        slots, here = rows_of(u)
        return remote(
            part.at[1 - y, slots, here], ybuf.at[slots, here],
            y_send.at[u], y_recv.at[u], (across, head),
        )

    def scatter(u, d):
        return remote(
            zpart.at[block_of(u, lax.rem(z + d, depth))], zbuf.at[(d,) + buffer_of(u)],
            z_send.at[u, d], z_recv.at[u, d], (along(d), head),
        )

    def gather(u, d):
        block = grad.at[(pl.ds(y * count, count),) + block_of(u, z)]
        return remote(block, block, a_send.at[u, d], a_recv.at[u, d], (along(d), head))

    def share(u):
        block = grad.at[(pl.ds(y * count, count),) + rows_of(u)]
        return remote(block, block, b_send.at[u], b_recv.at[u], (across, head))

    def scatter_all(u, far_y, d):
        i = far_y * depth + d
        return remote(
            part.at[(side(far_y),) + block_of(u, lax.rem(z + d, depth))], dbuf.at[i],
            d_send.at[i], d_recv.at[i], (other_dp(far_y, d), head),
        )

    def gather_all(u, far_y, d):
        i = far_y * depth + d
        block = grad.at[(pl.ds(y * count, count),) + block_of(u, z)]
        return remote(
            block, block, e_send.at[u, i], e_recv.at[u, i], (other_dp(far_y, d), head)
        )

    def multiply(s, row, rows, k=None):
        tokens = pl.ds(0, capacity) if k is None else pl.ds(k * span, span)
        here = pl.ds(row, rows)
        lhs = jnp.concatenate([lat_t[i, here, tokens] for i in s], axis=0)
        for j in range(2):
            value = dot_f32(lhs, vg_v[tokens, pl.ds(j * half, half)], ((1,), (0,)))
            for n, i in enumerate(s):
                mine = value[n * rows : (n + 1) * rows]
                if k:
                    mine = mine + acc[j, source[i], here, :]
                acc[j, source[i], here, :] = mine
                if k is None or k == TOKEN_PARTS - 1:
                    part[j, source[i], here, :] = mine.astype(jnp.bfloat16)

    def stage_z(u):
        here = rows_of(u)
        swap(u).wait_recv()
        total = acc[(y,) + here] + ybuf[here].astype(jnp.float32)
        zacc[here] = total
        zpart[here] = total.astype(jnp.bfloat16)
        for d in range(1, depth):
            scatter(u, d).start()

    def stage_gather(u):
        total = zacc[block_of(u, z)]
        for d in range(1, depth):
            scatter(u, d).wait_recv()
            total = total + zbuf[(d,) + buffer_of(u)].astype(jnp.float32)
        keep(u, total)
        if u == 0:
            for d in range(1, depth):
                gather(u, d).start()
        else:
            for o in others:
                gather_all(u, *o).start()

    def keep(u, total):
        for h in range(count):
            columns = total[..., h * V_DIM : (h + 1) * V_DIM]
            grad[(y * count + h,) + block_of(u, z)] = columns.astype(jnp.bfloat16)

    def reduce_all(u):
        total = acc[(y,) + block_of(u, z)]
        for o in others:
            scatter_all(u, *o).wait_recv()
            total = total + dbuf[o[0] * depth + o[1]].astype(jnp.float32)
        keep(u, total)
        for o in others:
            gather_all(u, *o).start()

    def stage_share(u):
        for d in range(1, depth):
            gather(u, d).wait_recv()
        share(u).start()

    def arrive(i):
        over[i].wait_recv()
        forward[i].start()

    last = len(units) - 1

    def multiply_piece(i):
        c, k = pieces[i]
        forward[i].wait_recv()
        multiply([2, 3], c * part_rows, part_rows, k)
        if i == TOKEN_PARTS - 1:
            swap(1).start()

    loads[2].wait()
    near.wait_recv()
    for k in range(TOKEN_PARTS):
        multiply([0, 1], 0, lat_cols, k)
        if k == 0:
            arrive(0)
    swap(0).start()
    for i in range(1, len(pieces)):
        arrive(i)
        if i == len(pieces) - 1:
            stage_gather(0)
        multiply_piece(i - 1)
        if i == len(pieces) // 2:
            stage_z(0)
    stage_z(1)
    multiply_piece(len(pieces) - 1)
    for o in others:
        scatter_all(last, *o).start()
    stage_share(0)
    stage_gather(1)
    reduce_all(last)
    share(0).wait_recv()
    for u in range(1, last + 1):
        for o in others:
            gather_all(u, *o).wait_recv()

    near.wait_send()
    for i in range(len(pieces)):
        over[i].wait_send()
        forward[i].wait_send()
    for o in others:
        scatter_all(last, *o).wait_send()
        for u in range(1, last + 1):
            gather_all(u, *o).wait_send()
    share(0).wait_send()
    for d in range(1, depth):
        gather(0, d).wait_send()
    for u in range(last):
        swap(u).wait_send()
        for d in range(1, depth):
            scatter(u, d).wait_send()


def kernel_body(depth, latent, value_grad, lengths):
    capacity, lat_cols = latent.shape
    width = value_grad.shape[1]
    half = width // 2
    units, pieces = ROW_PARTS, ROW_PARTS * TOKEN_PARTS
    dma = pltpu.SemaphoreType.DMA
    low, full = jnp.bfloat16, jnp.float32
    latent, value_grad, lengths = (
        pltpu.with_memory_space_constraint(a, pltpu.HBM) for a in (latent, value_grad, lengths)
    )
    sums = pl.pallas_call(
        functools.partial(kernel, depth),
        out_shape=pltpu.VMEM((width // V_DIM, 4, lat_cols, V_DIM), low),
        in_specs=[pl.BlockSpec(memory_space=pltpu.HBM)] * 3,
        out_specs=pl.BlockSpec(memory_space=pltpu.VMEM),
        scratch_shapes=[
            pltpu.SMEM(lengths.shape, jnp.int32),
            pltpu.VMEM((capacity, lat_cols), low),
            pltpu.VMEM((capacity, width), low),
            pltpu.VMEM((4, lat_cols, capacity), low),
            pltpu.VMEM((2, 4, lat_cols, half), full),
            pltpu.VMEM((2, 4, lat_cols, half), low),
            pltpu.VMEM((4, lat_cols, half), low),
            pltpu.VMEM((4, lat_cols, half), full),
            pltpu.VMEM((4, lat_cols, half), low),
            pltpu.VMEM((depth, 4, lat_cols // depth, half), low),
            pltpu.VMEM((2 * depth, 2, lat_cols // ROW_PARTS // depth, half), low),
            dma((3,)), dma((2,)),
            dma((pieces,)), dma((pieces,)), dma((pieces,)), dma((pieces,)),
            dma((units,)), dma((units,)),
            dma((units, depth)), dma((units, depth)),
            dma((units, depth)), dma((units, depth)),
            dma((units,)), dma((units,)),
            dma((2 * depth,)), dma((2 * depth,)), dma((1 + units, 2 * depth)), dma((1 + units, 2 * depth)),
        ],
        compiler_params=pltpu.CompilerParams(
            collective_id=0, has_side_effects=True, vmem_limit_bytes=48 * 2**20
        ),
        name="gradient_sums",
    )(lengths, latent, value_grad)
    return newton_schulz(sums.reshape(width // V_DIM, KV_RANK, V_DIM))


def solution(mesh):
    n_dp, n_head = mesh.shape["dp"], mesh.shape["head"]
    depth = n_dp // 2
    fits = n_head == 4 and KV_RANK // n_head == 16 * ROW_PARTS * depth
    body = functools.partial(kernel_body, depth) if fits else plain_body
    return jax.shard_map(
        body,
        mesh=mesh,
        in_specs=(P("dp", "head"), P("dp", "head"), P()),
        out_specs=P("head", None, None),
        check_vma=False,
    )
```

```python
import functools

import jax
import jax.numpy as jnp
from jax import lax
from jax.experimental import pallas as pl
from jax.experimental.pallas import tpu as pltpu
from jax.sharding import PartitionSpec as P

KV_RANK = 512
V_DIM = 128
ITERS = 5
ROW_PARTS = 2
TOKEN_PARTS = 3

epsilon = 1e-07
coef_one = 3.4445
coef_two = -4.775
coef_three = 2.0315


def plain_body(latent, value_grad, lengths):
    capacity, lat_cols = latent.shape
    grad_width = value_grad.shape[1]
    head_count = grad_width // V_DIM
    my_index = lax.axis_index("dp")
    own_length = lengths[my_index]
    slot_live = jnp.arange(capacity, dtype=jnp.int32) < own_length
    rows_grad = jnp.where(slot_live[:, None], value_grad, jnp.zeros_like(value_grad))
    partial_sum = lax.dot_general(
        lax.all_gather(latent, "head", axis=1, tiled=True),
        rows_grad,
        (((0,), (0,)), ((), ())),
        preferred_element_type=jnp.float32,
    )
    dw_shard = lax.psum_scatter(partial_sum, "dp", scatter_dimension=0, tiled=True)
    shard_heads = dw_shard.reshape(dw_shard.shape[0], head_count, V_DIM)
    local_squares = jnp.sum(shard_heads * shard_heads, axis=(0, 2))
    square_total = lax.psum(local_squares, "dp")
    head_norm = jnp.sqrt(square_total)
    ortho_shard = (shard_heads / (head_norm[None, :, None] + epsilon)).astype(jnp.bfloat16)
    ortho = lax.all_gather(ortho_shard, "dp", axis=0, tiled=True)
    for step in range(ITERS):
        gram_mat = jnp.einsum(
            "rhv,rhw->hvw", ortho, ortho, preferred_element_type=jnp.float32
        ).astype(jnp.bfloat16)
        squared = jnp.einsum("hvu,huw->hvw", gram_mat, gram_mat, preferred_element_type=jnp.float32)
        poly_mat = (coef_two * gram_mat.astype(jnp.float32) + coef_three * squared).astype(
            jnp.bfloat16
        )
        product = jnp.einsum("rhv,hvw->rhw", ortho, poly_mat, preferred_element_type=jnp.float32)
        ortho = (coef_one * ortho.astype(jnp.float32) + product).astype(jnp.bfloat16)
    scale = 0.2 * max(KV_RANK, V_DIM) ** 0.5
    update = (scale * ortho.astype(jnp.float32)).astype(jnp.bfloat16)
    return jnp.transpose(update, (1, 0, 2))


def dot_f32(a, b, dims):
    return lax.dot_general(a, b, (dims, ((), ())), preferred_element_type=jnp.float32)


def newton_schulz(grads):
    wide = grads.astype(jnp.float32)
    inv = 1.0 / (jnp.sqrt(jnp.sum(wide * wide, axis=(1, 2), keepdims=True)) + epsilon)
    ortho = grads
    for step in range(ITERS):
        gram = jnp.einsum("hrv,hrw->hvw", ortho, ortho, preferred_element_type=jnp.float32)
        if step == 0:
            gram = gram * inv * inv
        gram = gram.astype(jnp.bfloat16)
        squared = jnp.einsum("hvu,huw->hvw", gram, gram, preferred_element_type=jnp.float32)
        poly = (coef_two * gram.astype(jnp.float32) + coef_three * squared).astype(jnp.bfloat16)
        product = jnp.einsum("hrv,hvw->hrw", ortho, poly, preferred_element_type=jnp.float32)
        wide = coef_one * ortho.astype(jnp.float32) + product
        if step == 0:
            wide = wide * inv
        ortho = wide.astype(jnp.bfloat16)
    scale = 0.2 * max(KV_RANK, V_DIM) ** 0.5
    return (scale * ortho.astype(jnp.float32)).astype(jnp.bfloat16)


def kernel(
    depth,
    len_hbm, lat_hbm, vg_hbm, grad,
    len_s, lat_v, vg_v, lat_t, acc, part, ybuf, zacc, zpart, zbuf, dbuf,
    load_sem, sib_sem, x_send, x_recv, f_send, f_recv,
    y_send, y_recv, z_send, z_recv, a_send, a_recv, b_send, b_recv,
    d_send, d_recv, e_send, e_recv,
):
    dp = lax.axis_index("dp")
    head = lax.axis_index("head")
    y, z = lax.rem(dp, 2), lax.div(dp, 2)
    core = lax.rem(head, 2)
    sibling = head + 1 - 2 * core
    partner = lax.rem(head + 2, 4)
    far = lax.rem(sibling + 2, 4)
    source = (head, sibling, partner, far)
    across = dp + 1 - 2 * y
    lat_cols, capacity = lat_t.shape[1], lat_t.shape[2]
    half = acc.shape[3]
    count = half // V_DIM
    part_rows = lat_cols // ROW_PARTS
    span = capacity // TOKEN_PARTS

    def along(d):
        return lax.rem(z + d, depth) * 2 + y

    def side(far_y):
        return 1 - y if far_y else y

    def other_dp(far_y, d):
        return lax.rem(z + d, depth) * 2 + side(far_y)

    loads = [
        pltpu.make_async_copy(src, dst, load_sem.at[i])
        for i, (src, dst) in enumerate(((lat_hbm, lat_v), (len_hbm, len_s), (vg_hbm, vg_v)))
    ]
    for c in loads:
        c.start()

    barrier = pltpu.get_barrier_semaphore()
    others = [(far_y, d) for far_y in range(2) for d in range(depth) if far_y or d]
    friends = [(dp, sibling), (dp, partner)]
    friends += [(other_dp(*o), head) for o in others]
    for where in friends:
        pl.semaphore_signal(barrier, inc=1, device_id=where, device_id_type=pl.DeviceIdType.MESH)

    loads[0].wait()
    loads[1].wait()

    def turn(k):
        tokens = pl.ds(k * span, span)
        turned = lat_v[tokens, :].T
        live = lax.broadcasted_iota(jnp.int32, turned.shape, 1) + k * span < len_s[dp]
        lat_t[0, :, tokens] = jnp.where(live, turned, jnp.zeros_like(turned))

    turn(0)
    pl.semaphore_wait(barrier, len(friends))

    def remote(src, dst, ssem, rsem, where):
        return pltpu.make_async_remote_copy(
            src_ref=src, dst_ref=dst, send_sem=ssem, recv_sem=rsem,
            device_id=where, device_id_type=pl.DeviceIdType.MESH,
        )

    pieces = [(c, k) for c in range(ROW_PARTS) for k in range(TOKEN_PARTS)]

    def piece(slot, i):
        c, k = pieces[i]
        return lat_t.at[slot, pl.ds(c * part_rows, part_rows), pl.ds(k * span, span)]

    over = [
        remote(piece(0, i), piece(2, i), x_send.at[i], x_recv.at[i], (dp, partner))
        for i in range(len(pieces))
    ]
    forward = [
        remote(piece(2, i), piece(3, i), f_send.at[i], f_recv.at[i], (dp, sibling))
        for i in range(len(pieces))
    ]
    near = remote(lat_t.at[0], lat_t.at[1], sib_sem.at[0], sib_sem.at[1], (dp, sibling))
    over[0].start()
    for k in range(1, TOKEN_PARTS):
        turn(k)
    near.start()
    over[1].start()

    own, other = head - core, partner - core
    units = [(own, 0, lat_cols)]
    units += [(other, c * part_rows, part_rows) for c in range(ROW_PARTS)]

    def rows_of(u):
        s, row, rows = units[u]
        return pl.ds(s, 2), pl.ds(row, rows)

    def block_of(u, zz):
        s, row, rows = units[u]
        block = rows // depth
        return pl.ds(s, 2), pl.ds(pl.multiple_of(row + zz * block, block), block)

    def buffer_of(u):
        s, row, rows = units[u]
        return pl.ds(s, 2), pl.ds(row // depth, rows // depth)

    def swap(u):
        slots, here = rows_of(u)
        return remote(
            part.at[1 - y, slots, here], ybuf.at[slots, here],
            y_send.at[u], y_recv.at[u], (across, head),
        )

    def scatter(u, d):
        return remote(
            zpart.at[block_of(u, lax.rem(z + d, depth))], zbuf.at[(d,) + buffer_of(u)],
            z_send.at[u, d], z_recv.at[u, d], (along(d), head),
        )

    def gather(u, d):
        block = grad.at[(pl.ds(y * count, count),) + block_of(u, z)]
        return remote(block, block, a_send.at[u, d], a_recv.at[u, d], (along(d), head))

    def share(u):
        block = grad.at[(pl.ds(y * count, count),) + rows_of(u)]
        return remote(block, block, b_send.at[u], b_recv.at[u], (across, head))

    def scatter_all(u, far_y, d):
        i = far_y * depth + d
        return remote(
            part.at[(side(far_y),) + block_of(u, lax.rem(z + d, depth))], dbuf.at[i],
            d_send.at[i], d_recv.at[i], (other_dp(far_y, d), head),
        )

    def gather_all(u, far_y, d):
        i = far_y * depth + d
        block = grad.at[(pl.ds(y * count, count),) + block_of(u, z)]
        return remote(block, block, e_send.at[i], e_recv.at[i], (other_dp(far_y, d), head))

    def multiply(s, row, rows, k=None):
        tokens = pl.ds(0, capacity) if k is None else pl.ds(k * span, span)
        here = pl.ds(row, rows)
        lhs = jnp.concatenate([lat_t[i, here, tokens] for i in s], axis=0)
        for j in range(2):
            value = dot_f32(lhs, vg_v[tokens, pl.ds(j * half, half)], ((1,), (0,)))
            for n, i in enumerate(s):
                mine = value[n * rows : (n + 1) * rows]
                if k:
                    mine = mine + acc[j, source[i], here, :]
                acc[j, source[i], here, :] = mine
                if k is None or k == TOKEN_PARTS - 1:
                    part[j, source[i], here, :] = mine.astype(jnp.bfloat16)

    def stage_z(u):
        here = rows_of(u)
        swap(u).wait_recv()
        total = acc[(y,) + here] + ybuf[here].astype(jnp.float32)
        zacc[here] = total
        zpart[here] = total.astype(jnp.bfloat16)
        for d in range(1, depth):
            scatter(u, d).start()

    def stage_gather(u):
        total = zacc[block_of(u, z)]
        for d in range(1, depth):
            scatter(u, d).wait_recv()
            total = total + zbuf[(d,) + buffer_of(u)].astype(jnp.float32)
        keep(u, total)
        for d in range(1, depth):
            gather(u, d).start()

    def keep(u, total):
        for h in range(count):
            columns = total[..., h * V_DIM : (h + 1) * V_DIM]
            grad[(y * count + h,) + block_of(u, z)] = columns.astype(jnp.bfloat16)

    def reduce_all(u):
        total = acc[(y,) + block_of(u, z)]
        for o in others:
            scatter_all(u, *o).wait_recv()
            total = total + dbuf[o[0] * depth + o[1]].astype(jnp.float32)
        keep(u, total)
        for o in others:
            gather_all(u, *o).start()

    def stage_share(u):
        for d in range(1, depth):
            gather(u, d).wait_recv()
        share(u).start()

    def arrive(i):
        over[i].wait_recv()
        forward[i].start()
        if i + 2 < len(pieces):
            over[i + 2].start()

    last = len(units) - 1

    def multiply_piece(i):
        c, k = pieces[i]
        forward[i].wait_recv()
        multiply([2, 3], c * part_rows, part_rows, k)
        if i == TOKEN_PARTS - 1:
            swap(1).start()

    loads[2].wait()
    near.wait_recv()
    for k in range(TOKEN_PARTS):
        multiply([0, 1], 0, lat_cols, k)
        if k == 0:
            arrive(0)
    swap(0).start()
    for i in range(1, len(pieces)):
        arrive(i)
        multiply_piece(i - 1)
        if i == len(pieces) - 2:
            stage_z(0)
    stage_z(1)
    multiply_piece(len(pieces) - 1)
    for o in others:
        scatter_all(last, *o).start()
    stage_gather(0)
    stage_gather(1)
    reduce_all(last)
    stage_share(0)
    stage_share(1)
    for u in range(last):
        share(u).wait_recv()
    for o in others:
        gather_all(last, *o).wait_recv()

    near.wait_send()
    for i in range(len(pieces)):
        over[i].wait_send()
        forward[i].wait_send()
    for o in others:
        scatter_all(last, *o).wait_send()
        gather_all(last, *o).wait_send()
    for u in range(last):
        swap(u).wait_send()
        share(u).wait_send()
        for d in range(1, depth):
            scatter(u, d).wait_send()
            gather(u, d).wait_send()


def kernel_body(depth, latent, value_grad, lengths):
    capacity, lat_cols = latent.shape
    width = value_grad.shape[1]
    half = width // 2
    units, pieces = ROW_PARTS, ROW_PARTS * TOKEN_PARTS
    dma = pltpu.SemaphoreType.DMA
    low, full = jnp.bfloat16, jnp.float32
    latent, value_grad, lengths = (
        pltpu.with_memory_space_constraint(a, pltpu.HBM) for a in (latent, value_grad, lengths)
    )
    sums = pl.pallas_call(
        functools.partial(kernel, depth),
        out_shape=pltpu.VMEM((width // V_DIM, 4, lat_cols, V_DIM), low),
        in_specs=[pl.BlockSpec(memory_space=pltpu.HBM)] * 3,
        out_specs=pl.BlockSpec(memory_space=pltpu.VMEM),
        scratch_shapes=[
            pltpu.SMEM(lengths.shape, jnp.int32),
            pltpu.VMEM((capacity, lat_cols), low),
            pltpu.VMEM((capacity, width), low),
            pltpu.VMEM((4, lat_cols, capacity), low),
            pltpu.VMEM((2, 4, lat_cols, half), full),
            pltpu.VMEM((2, 4, lat_cols, half), low),
            pltpu.VMEM((4, lat_cols, half), low),
            pltpu.VMEM((4, lat_cols, half), full),
            pltpu.VMEM((4, lat_cols, half), low),
            pltpu.VMEM((depth, 4, lat_cols // depth, half), low),
            pltpu.VMEM((2 * depth, 2, lat_cols // ROW_PARTS // depth, half), low),
            dma((3,)), dma((2,)),
            dma((pieces,)), dma((pieces,)), dma((pieces,)), dma((pieces,)),
            dma((units,)), dma((units,)),
            dma((units, depth)), dma((units, depth)),
            dma((units, depth)), dma((units, depth)),
            dma((units,)), dma((units,)),
            dma((2 * depth,)), dma((2 * depth,)), dma((2 * depth,)), dma((2 * depth,)),
        ],
        compiler_params=pltpu.CompilerParams(
            collective_id=0, has_side_effects=True, vmem_limit_bytes=48 * 2**20
        ),
        name="gradient_sums",
    )(lengths, latent, value_grad)
    return newton_schulz(sums.reshape(width // V_DIM, KV_RANK, V_DIM))


def solution(mesh):
    n_dp, n_head = mesh.shape["dp"], mesh.shape["head"]
    depth = n_dp // 2
    fits = n_head == 4 and KV_RANK // n_head == 16 * ROW_PARTS * depth
    body = functools.partial(kernel_body, depth) if fits else plain_body
    return jax.shard_map(
        body,
        mesh=mesh,
        in_specs=(P("dp", "head"), P("dp", "head"), P()),
        out_specs=P("head", None, None),
        check_vma=False,
    )
```

```python
import functools

import jax
import jax.numpy as jnp
from jax import lax
from jax.experimental import pallas as pl
from jax.experimental.pallas import tpu as pltpu
from jax.sharding import PartitionSpec as P

KV_RANK = 512
V_DIM = 128
ITERS = 5
ROW_PARTS = 2
TOKEN_PARTS = 3

epsilon = 1e-07
coef_one = 3.4445
coef_two = -4.775
coef_three = 2.0315


def plain_body(latent, value_grad, lengths):
    capacity, lat_cols = latent.shape
    grad_width = value_grad.shape[1]
    head_count = grad_width // V_DIM
    my_index = lax.axis_index("dp")
    own_length = lengths[my_index]
    slot_live = jnp.arange(capacity, dtype=jnp.int32) < own_length
    rows_grad = jnp.where(slot_live[:, None], value_grad, jnp.zeros_like(value_grad))
    partial_sum = lax.dot_general(
        lax.all_gather(latent, "head", axis=1, tiled=True),
        rows_grad,
        (((0,), (0,)), ((), ())),
        preferred_element_type=jnp.float32,
    )
    dw_shard = lax.psum_scatter(partial_sum, "dp", scatter_dimension=0, tiled=True)
    shard_heads = dw_shard.reshape(dw_shard.shape[0], head_count, V_DIM)
    local_squares = jnp.sum(shard_heads * shard_heads, axis=(0, 2))
    square_total = lax.psum(local_squares, "dp")
    head_norm = jnp.sqrt(square_total)
    ortho_shard = (shard_heads / (head_norm[None, :, None] + epsilon)).astype(jnp.bfloat16)
    ortho = lax.all_gather(ortho_shard, "dp", axis=0, tiled=True)
    for step in range(ITERS):
        gram_mat = jnp.einsum(
            "rhv,rhw->hvw", ortho, ortho, preferred_element_type=jnp.float32
        ).astype(jnp.bfloat16)
        squared = jnp.einsum("hvu,huw->hvw", gram_mat, gram_mat, preferred_element_type=jnp.float32)
        poly_mat = (coef_two * gram_mat.astype(jnp.float32) + coef_three * squared).astype(
            jnp.bfloat16
        )
        product = jnp.einsum("rhv,hvw->rhw", ortho, poly_mat, preferred_element_type=jnp.float32)
        ortho = (coef_one * ortho.astype(jnp.float32) + product).astype(jnp.bfloat16)
    scale = 0.2 * max(KV_RANK, V_DIM) ** 0.5
    update = (scale * ortho.astype(jnp.float32)).astype(jnp.bfloat16)
    return jnp.transpose(update, (1, 0, 2))


def dot_f32(a, b, dims):
    return lax.dot_general(a, b, (dims, ((), ())), preferred_element_type=jnp.float32)


def newton_schulz(grads):
    wide = grads.astype(jnp.float32)
    inv = 1.0 / (jnp.sqrt(jnp.sum(wide * wide, axis=(1, 2), keepdims=True)) + epsilon)
    ortho = grads
    for step in range(ITERS):
        gram = jnp.einsum("hrv,hrw->hvw", ortho, ortho, preferred_element_type=jnp.float32)
        if step == 0:
            gram = gram * inv * inv
        gram = gram.astype(jnp.bfloat16)
        squared = jnp.einsum("hvu,huw->hvw", gram, gram, preferred_element_type=jnp.float32)
        poly = (coef_two * gram.astype(jnp.float32) + coef_three * squared).astype(jnp.bfloat16)
        product = jnp.einsum("hrv,hvw->hrw", ortho, poly, preferred_element_type=jnp.float32)
        wide = coef_one * ortho.astype(jnp.float32) + product
        if step == 0:
            wide = wide * inv
        ortho = wide.astype(jnp.bfloat16)
    scale = 0.2 * max(KV_RANK, V_DIM) ** 0.5
    return (scale * ortho.astype(jnp.float32)).astype(jnp.bfloat16)


def kernel(
    depth,
    len_hbm, lat_hbm, vg_hbm, grad,
    len_s, lat_v, vg_v, lat_t, acc, part, dbuf,
    load_sem, sib_sem, x_send, x_recv, f_send, f_recv,
    d_send, d_recv, e_send, e_recv,
):
    dp = lax.axis_index("dp")
    head = lax.axis_index("head")
    y, z = lax.rem(dp, 2), lax.div(dp, 2)
    core = lax.rem(head, 2)
    sibling = head + 1 - 2 * core
    partner = lax.rem(head + 2, 4)
    far = lax.rem(sibling + 2, 4)
    source = (head, sibling, partner, far)
    lat_cols, capacity = lat_t.shape[1], lat_t.shape[2]
    half = acc.shape[3]
    count = half // V_DIM
    part_rows = lat_cols // ROW_PARTS
    span = capacity // TOKEN_PARTS

    def side(far_y):
        return 1 - y if far_y else y

    def other_dp(far_y, d):
        return lax.rem(z + d, depth) * 2 + side(far_y)

    loads = [
        pltpu.make_async_copy(src, dst, load_sem.at[i])
        for i, (src, dst) in enumerate(((lat_hbm, lat_v), (len_hbm, len_s), (vg_hbm, vg_v)))
    ]
    for c in loads:
        c.start()

    barrier = pltpu.get_barrier_semaphore()
    others = [(far_y, d) for far_y in range(2) for d in range(depth) if far_y or d]
    friends = [(dp, sibling), (dp, partner)]
    friends += [(other_dp(*o), head) for o in others]
    for where in friends:
        pl.semaphore_signal(barrier, inc=1, device_id=where, device_id_type=pl.DeviceIdType.MESH)

    loads[0].wait()
    loads[1].wait()

    def turn(k):
        tokens = pl.ds(k * span, span)
        turned = lat_v[tokens, :].T
        live = lax.broadcasted_iota(jnp.int32, turned.shape, 1) + k * span < len_s[dp]
        lat_t[0, :, tokens] = jnp.where(live, turned, jnp.zeros_like(turned))

    turn(0)
    pl.semaphore_wait(barrier, len(friends))

    def remote(src, dst, ssem, rsem, where):
        return pltpu.make_async_remote_copy(
            src_ref=src, dst_ref=dst, send_sem=ssem, recv_sem=rsem,
            device_id=where, device_id_type=pl.DeviceIdType.MESH,
        )

    pieces = [(c, k) for c in range(ROW_PARTS) for k in range(TOKEN_PARTS)]

    def piece(slot, i):
        c, k = pieces[i]
        return lat_t.at[slot, pl.ds(c * part_rows, part_rows), pl.ds(k * span, span)]

    over = [
        remote(piece(0, i), piece(2, i), x_send.at[i], x_recv.at[i], (dp, partner))
        for i in range(len(pieces))
    ]
    forward = [
        remote(piece(2, i), piece(3, i), f_send.at[i], f_recv.at[i], (dp, sibling))
        for i in range(len(pieces))
    ]
    near = remote(lat_t.at[0], lat_t.at[1], sib_sem.at[0], sib_sem.at[1], (dp, sibling))
    over[0].start()
    for k in range(1, TOKEN_PARTS):
        turn(k)
    near.start()
    over[1].start()

    own, other = head - core, partner - core
    units = [(own, 0, lat_cols)]
    units += [(other, c * part_rows, part_rows) for c in range(ROW_PARTS)]

    def block_of(u, zz):
        s, row, rows = units[u]
        block = rows // depth
        return pl.ds(s, 2), pl.ds(pl.multiple_of(row + zz * block, block), block)

    def buffer_of(u):
        s, row, rows = units[u]
        return pl.ds(s, 2), pl.ds(row // depth, rows // depth)

    def scatter_all(u, far_y, d):
        i = far_y * depth + d
        return remote(
            part.at[(side(far_y),) + block_of(u, lax.rem(z + d, depth))], dbuf.at[(i,) + buffer_of(u)],
            d_send.at[u, i], d_recv.at[u, i], (other_dp(far_y, d), head),
        )

    def gather_all(u, far_y, d):
        i = far_y * depth + d
        block = grad.at[(pl.ds(y * count, count),) + block_of(u, z)]
        return remote(block, block, e_send.at[u, i], e_recv.at[u, i], (other_dp(far_y, d), head))

    def multiply(s, row, rows, k=None):
        tokens = pl.ds(0, capacity) if k is None else pl.ds(k * span, span)
        here = pl.ds(row, rows)
        lhs = jnp.concatenate([lat_t[i, here, tokens] for i in s], axis=0)
        for j in range(2):
            value = dot_f32(lhs, vg_v[tokens, pl.ds(j * half, half)], ((1,), (0,)))
            for n, i in enumerate(s):
                mine = value[n * rows : (n + 1) * rows]
                if k:
                    mine = mine + acc[j, source[i], here, :]
                acc[j, source[i], here, :] = mine
                if k is None or k == TOKEN_PARTS - 1:
                    part[j, source[i], here, :] = mine.astype(jnp.bfloat16)

    def keep(u, total):
        for h in range(count):
            columns = total[..., h * V_DIM : (h + 1) * V_DIM]
            grad[(y * count + h,) + block_of(u, z)] = columns.astype(jnp.bfloat16)

    def reduce_all(u):
        total = acc[(y,) + block_of(u, z)]
        for o in others:
            scatter_all(u, *o).wait_recv()
            total = total + dbuf[(o[0] * depth + o[1],) + buffer_of(u)].astype(jnp.float32)
        keep(u, total)
        for o in others:
            gather_all(u, *o).start()

    def arrive(i):
        over[i].wait_recv()
        forward[i].start()
        if i + 2 < len(pieces):
            over[i + 2].start()

    def scatter_unit(u):
        for o in others:
            scatter_all(u, *o).start()

    def multiply_piece(i):
        c, k = pieces[i]
        forward[i].wait_recv()
        multiply([2, 3], c * part_rows, part_rows, k)
        if i == TOKEN_PARTS - 1:
            scatter_unit(1)

    loads[2].wait()
    near.wait_recv()
    for k in range(TOKEN_PARTS):
        multiply([0, 1], 0, lat_cols, k)
        if k == 0:
            arrive(0)
    scatter_unit(0)
    for i in range(1, len(pieces)):
        arrive(i)
        multiply_piece(i - 1)
        if i == len(pieces) - 2:
            reduce_all(0)
    multiply_piece(len(pieces) - 1)
    scatter_unit(2)
    reduce_all(1)
    reduce_all(2)
    for u in range(len(units)):
        for o in others:
            gather_all(u, *o).wait_recv()

    near.wait_send()
    for i in range(len(pieces)):
        over[i].wait_send()
        forward[i].wait_send()
    for u in range(len(units)):
        for o in others:
            scatter_all(u, *o).wait_send()
            gather_all(u, *o).wait_send()


def kernel_body(depth, latent, value_grad, lengths):
    capacity, lat_cols = latent.shape
    width = value_grad.shape[1]
    half = width // 2
    units, pieces = 1 + ROW_PARTS, ROW_PARTS * TOKEN_PARTS
    dma = pltpu.SemaphoreType.DMA
    low, full = jnp.bfloat16, jnp.float32
    latent, value_grad, lengths = (
        pltpu.with_memory_space_constraint(a, pltpu.HBM) for a in (latent, value_grad, lengths)
    )
    sums = pl.pallas_call(
        functools.partial(kernel, depth),
        out_shape=pltpu.VMEM((width // V_DIM, 4, lat_cols, V_DIM), low),
        in_specs=[pl.BlockSpec(memory_space=pltpu.HBM)] * 3,
        out_specs=pl.BlockSpec(memory_space=pltpu.VMEM),
        scratch_shapes=[
            pltpu.SMEM(lengths.shape, jnp.int32),
            pltpu.VMEM((capacity, lat_cols), low),
            pltpu.VMEM((capacity, width), low),
            pltpu.VMEM((4, lat_cols, capacity), low),
            pltpu.VMEM((2, 4, lat_cols, half), full),
            pltpu.VMEM((2, 4, lat_cols, half), low),
            pltpu.VMEM((2 * depth, 4, lat_cols // depth, half), low),
            dma((3,)), dma((2,)),
            dma((pieces,)), dma((pieces,)), dma((pieces,)), dma((pieces,)),
            dma((units, 2 * depth)), dma((units, 2 * depth)), dma((units, 2 * depth)), dma((units, 2 * depth)),
        ],
        compiler_params=pltpu.CompilerParams(
            collective_id=0, has_side_effects=True, vmem_limit_bytes=48 * 2**20
        ),
        name="gradient_sums",
    )(lengths, latent, value_grad)
    return newton_schulz(sums.reshape(width // V_DIM, KV_RANK, V_DIM))


def solution(mesh):
    n_dp, n_head = mesh.shape["dp"], mesh.shape["head"]
    depth = n_dp // 2
    fits = n_head == 4 and KV_RANK // n_head == 16 * ROW_PARTS * depth
    body = functools.partial(kernel_body, depth) if fits else plain_body
    return jax.shard_map(
        body,
        mesh=mesh,
        in_specs=(P("dp", "head"), P("dp", "head"), P()),
        out_specs=P("head", None, None),
        check_vma=False,
    )
```

```python
import functools

import jax
import jax.numpy as jnp
from jax import lax
from jax.experimental import pallas as pl
from jax.experimental.pallas import tpu as pltpu
from jax.sharding import PartitionSpec as P

KV_RANK = 512
V_DIM = 128
ITERS = 5
ROW_PARTS = 2
TOKEN_PARTS = 3

epsilon = 1e-07
coef_one = 3.4445
coef_two = -4.775
coef_three = 2.0315


def plain_body(latent, value_grad, lengths):
    capacity, lat_cols = latent.shape
    grad_width = value_grad.shape[1]
    head_count = grad_width // V_DIM
    my_index = lax.axis_index("dp")
    own_length = lengths[my_index]
    slot_live = jnp.arange(capacity, dtype=jnp.int32) < own_length
    rows_grad = jnp.where(slot_live[:, None], value_grad, jnp.zeros_like(value_grad))
    partial_sum = lax.dot_general(
        lax.all_gather(latent, "head", axis=1, tiled=True),
        rows_grad,
        (((0,), (0,)), ((), ())),
        preferred_element_type=jnp.float32,
    )
    dw_shard = lax.psum_scatter(partial_sum, "dp", scatter_dimension=0, tiled=True)
    shard_heads = dw_shard.reshape(dw_shard.shape[0], head_count, V_DIM)
    local_squares = jnp.sum(shard_heads * shard_heads, axis=(0, 2))
    square_total = lax.psum(local_squares, "dp")
    head_norm = jnp.sqrt(square_total)
    ortho_shard = (shard_heads / (head_norm[None, :, None] + epsilon)).astype(jnp.bfloat16)
    ortho = lax.all_gather(ortho_shard, "dp", axis=0, tiled=True)
    for step in range(ITERS):
        gram_mat = jnp.einsum(
            "rhv,rhw->hvw", ortho, ortho, preferred_element_type=jnp.float32
        ).astype(jnp.bfloat16)
        squared = jnp.einsum("hvu,huw->hvw", gram_mat, gram_mat, preferred_element_type=jnp.float32)
        poly_mat = (coef_two * gram_mat.astype(jnp.float32) + coef_three * squared).astype(
            jnp.bfloat16
        )
        product = jnp.einsum("rhv,hvw->rhw", ortho, poly_mat, preferred_element_type=jnp.float32)
        ortho = (coef_one * ortho.astype(jnp.float32) + product).astype(jnp.bfloat16)
    scale = 0.2 * max(KV_RANK, V_DIM) ** 0.5
    update = (scale * ortho.astype(jnp.float32)).astype(jnp.bfloat16)
    return jnp.transpose(update, (1, 0, 2))


def dot_f32(a, b, dims):
    return lax.dot_general(a, b, (dims, ((), ())), preferred_element_type=jnp.float32)


def newton_schulz(grads):
    wide = grads.astype(jnp.float32)
    inv = 1.0 / (jnp.sqrt(jnp.sum(wide * wide, axis=(1, 2), keepdims=True)) + epsilon)
    ortho = grads
    for step in range(ITERS):
        gram = jnp.einsum("hrv,hrw->hvw", ortho, ortho, preferred_element_type=jnp.float32)
        if step == 0:
            gram = gram * inv * inv
        gram = gram.astype(jnp.bfloat16)
        squared = jnp.einsum("hvu,huw->hvw", gram, gram, preferred_element_type=jnp.float32)
        poly = (coef_two * gram.astype(jnp.float32) + coef_three * squared).astype(jnp.bfloat16)
        product = jnp.einsum("hrv,hvw->hrw", ortho, poly, preferred_element_type=jnp.float32)
        wide = coef_one * ortho.astype(jnp.float32) + product
        if step == 0:
            wide = wide * inv
        ortho = wide.astype(jnp.bfloat16)
    scale = 0.2 * max(KV_RANK, V_DIM) ** 0.5
    return (scale * ortho.astype(jnp.float32)).astype(jnp.bfloat16)


def kernel(
    depth,
    len_hbm, lat_hbm, vg_hbm, out_ref,
    len_s, lat_v, vg_v, lat_t, acc, part, ybuf, zacc, zpart, zbuf, dbuf, grad,
    load_sem, sib_sem, x_send, x_recv, f_send, f_recv,
    y_send, y_recv, z_send, z_recv, a_send, a_recv, b_send, b_recv,
    d_send, d_recv, e_send, e_recv,
):
    dp = lax.axis_index("dp")
    head = lax.axis_index("head")
    y, z = lax.rem(dp, 2), lax.div(dp, 2)
    core = lax.rem(head, 2)
    sibling = head + 1 - 2 * core
    partner = lax.rem(head + 2, 4)
    far = lax.rem(sibling + 2, 4)
    source = (head, sibling, partner, far)
    across = dp + 1 - 2 * y
    lat_cols, capacity = lat_t.shape[1], lat_t.shape[2]
    half = acc.shape[3]
    count = half // V_DIM
    part_rows = lat_cols // ROW_PARTS
    span = capacity // TOKEN_PARTS

    def along(d):
        return lax.rem(z + d, depth) * 2 + y

    def side(far_y):
        return 1 - y if far_y else y

    def other_dp(far_y, d):
        return lax.rem(z + d, depth) * 2 + side(far_y)

    loads = [
        pltpu.make_async_copy(src, dst, load_sem.at[i])
        for i, (src, dst) in enumerate(((lat_hbm, lat_v), (len_hbm, len_s), (vg_hbm, vg_v)))
    ]
    for c in loads:
        c.start()

    barrier = pltpu.get_barrier_semaphore()
    others = [(far_y, d) for far_y in range(2) for d in range(depth) if far_y or d]
    friends = [(dp, sibling), (dp, partner)]
    friends += [(other_dp(*o), head) for o in others]
    for where in friends:
        pl.semaphore_signal(barrier, inc=1, device_id=where, device_id_type=pl.DeviceIdType.MESH)

    loads[0].wait()
    loads[1].wait()

    def turn(k):
        tokens = pl.ds(k * span, span)
        turned = lat_v[tokens, :].T
        live = lax.broadcasted_iota(jnp.int32, turned.shape, 1) + k * span < len_s[dp]
        lat_t[0, :, tokens] = jnp.where(live, turned, jnp.zeros_like(turned))

    turn(0)
    pl.semaphore_wait(barrier, len(friends))

    def remote(src, dst, ssem, rsem, where):
        return pltpu.make_async_remote_copy(
            src_ref=src, dst_ref=dst, send_sem=ssem, recv_sem=rsem,
            device_id=where, device_id_type=pl.DeviceIdType.MESH,
        )

    pieces = [(c, k) for c in range(ROW_PARTS) for k in range(TOKEN_PARTS)]

    def piece(slot, i):
        c, k = pieces[i]
        return lat_t.at[slot, pl.ds(c * part_rows, part_rows), pl.ds(k * span, span)]

    over = [
        remote(piece(0, i), piece(2, i), x_send.at[i], x_recv.at[i], (dp, partner))
        for i in range(len(pieces))
    ]
    forward = [
        remote(piece(2, i), piece(3, i), f_send.at[i], f_recv.at[i], (dp, sibling))
        for i in range(len(pieces))
    ]
    near = remote(lat_t.at[0], lat_t.at[1], sib_sem.at[0], sib_sem.at[1], (dp, sibling))
    over[0].start()
    for k in range(1, TOKEN_PARTS):
        turn(k)
    near.start()
    for c in over[1:]:
        c.start()

    own, other = head - core, partner - core
    units = [(own, 0, lat_cols)]
    units += [(other, c * part_rows, part_rows) for c in range(ROW_PARTS)]

    def rows_of(u):
        s, row, rows = units[u]
        return pl.ds(s, 2), pl.ds(row, rows)

    def block_of(u, zz):
        s, row, rows = units[u]
        block = rows // depth
        return pl.ds(s, 2), pl.ds(pl.multiple_of(row + zz * block, block), block)

    def buffer_of(u):
        s, row, rows = units[u]
        return pl.ds(s, 2), pl.ds(row // depth, rows // depth)

    def swap(u):
        slots, here = rows_of(u)
        return remote(
            part.at[1 - y, slots, here], ybuf.at[slots, here],
            y_send.at[u], y_recv.at[u], (across, head),
        )

    def scatter(u, d):
        return remote(
            zpart.at[block_of(u, lax.rem(z + d, depth))], zbuf.at[(d,) + buffer_of(u)],
            z_send.at[u, d], z_recv.at[u, d], (along(d), head),
        )

    def gather(u, d):
        block = grad.at[(y,) + block_of(u, z)]
        return remote(block, block, a_send.at[u, d], a_recv.at[u, d], (along(d), head))

    def share(u):
        block = grad.at[(y,) + rows_of(u)]
        return remote(block, block, b_send.at[u], b_recv.at[u], (across, head))

    def scatter_all(u, far_y, d):
        i = far_y * depth + d
        return remote(
            part.at[(side(far_y),) + block_of(u, lax.rem(z + d, depth))], dbuf.at[i],
            d_send.at[i], d_recv.at[i], (other_dp(far_y, d), head),
        )

    def gather_all(u, far_y, d):
        i = far_y * depth + d
        block = grad.at[(y,) + block_of(u, z)]
        return remote(block, block, e_send.at[i], e_recv.at[i], (other_dp(far_y, d), head))

    def multiply(s, row, rows, k=None):
        tokens = pl.ds(0, capacity) if k is None else pl.ds(k * span, span)
        here = pl.ds(row, rows)
        lhs = jnp.concatenate([lat_t[i, here, tokens] for i in s], axis=0)
        for j in range(2):
            value = dot_f32(lhs, vg_v[tokens, pl.ds(j * half, half)], ((1,), (0,)))
            for n, i in enumerate(s):
                mine = value[n * rows : (n + 1) * rows]
                if k:
                    mine = mine + acc[j, source[i], here, :]
                acc[j, source[i], here, :] = mine
                if k is None or k == TOKEN_PARTS - 1:
                    part[j, source[i], here, :] = mine.astype(jnp.bfloat16)

    def stage_z(u):
        here = rows_of(u)
        swap(u).wait_recv()
        total = acc[(y,) + here] + ybuf[here].astype(jnp.float32)
        zacc[here] = total
        zpart[here] = total.astype(jnp.bfloat16)
        for d in range(1, depth):
            scatter(u, d).start()

    def stage_gather(u):
        total = zacc[block_of(u, z)]
        for d in range(1, depth):
            scatter(u, d).wait_recv()
            total = total + zbuf[(d,) + buffer_of(u)].astype(jnp.float32)
        keep(u, total)
        for d in range(1, depth):
            gather(u, d).start()

    def keep(u, total):
        grad[(y,) + block_of(u, z)] = total.astype(jnp.bfloat16)

    def reduce_all(u):
        total = acc[(y,) + block_of(u, z)]
        for o in others:
            scatter_all(u, *o).wait_recv()
            total = total + dbuf[o[0] * depth + o[1]].astype(jnp.float32)
        keep(u, total)
        for o in others:
            gather_all(u, *o).start()

    def stage_share(u):
        for d in range(1, depth):
            gather(u, d).wait_recv()
        share(u).start()

    def arrive(i):
        over[i].wait_recv()
        forward[i].start()

    last = len(units) - 1
    loads[2].wait()
    multiply([0], 0, lat_cols)
    near.wait_recv()
    multiply([1], 0, lat_cols)
    swap(0).start()
    for c in range(ROW_PARTS):
        for k in range(TOKEN_PARTS):
            i = c * TOKEN_PARTS + k
            arrive(i)
            if k == 1:
                stage_z(c)
            if c == 1 and k == 2:
                stage_gather(1)
            forward[i].wait_recv()
            multiply([2, 3], c * part_rows, part_rows, k)
        if c == 0:
            swap(1).start()
            stage_gather(0)
    for o in others:
        scatter_all(last, *o).start()
    stage_share(0)
    reduce_all(last)
    stage_share(1)
    for u in range(last):
        share(u).wait_recv()
    for o in others:
        gather_all(last, *o).wait_recv()
    for j in range(2):
        for h in range(count):
            out_ref[j * count + h] = grad[j, :, :, pl.ds(h * V_DIM, V_DIM)]

    near.wait_send()
    for i in range(len(pieces)):
        over[i].wait_send()
        forward[i].wait_send()
    for o in others:
        scatter_all(last, *o).wait_send()
        gather_all(last, *o).wait_send()
    for u in range(last):
        swap(u).wait_send()
        share(u).wait_send()
        for d in range(1, depth):
            scatter(u, d).wait_send()
            gather(u, d).wait_send()


def kernel_body(depth, latent, value_grad, lengths):
    capacity, lat_cols = latent.shape
    width = value_grad.shape[1]
    half = width // 2
    units, pieces = ROW_PARTS, ROW_PARTS * TOKEN_PARTS
    dma = pltpu.SemaphoreType.DMA
    low, full = jnp.bfloat16, jnp.float32
    latent, value_grad, lengths = (
        pltpu.with_memory_space_constraint(a, pltpu.HBM) for a in (latent, value_grad, lengths)
    )
    sums = pl.pallas_call(
        functools.partial(kernel, depth),
        out_shape=pltpu.VMEM((width // V_DIM, 4, lat_cols, V_DIM), low),
        in_specs=[pl.BlockSpec(memory_space=pltpu.HBM)] * 3,
        out_specs=pl.BlockSpec(memory_space=pltpu.VMEM),
        scratch_shapes=[
            pltpu.SMEM(lengths.shape, jnp.int32),
            pltpu.VMEM((capacity, lat_cols), low),
            pltpu.VMEM((capacity, width), low),
            pltpu.VMEM((4, lat_cols, capacity), low),
            pltpu.VMEM((2, 4, lat_cols, half), full),
            pltpu.VMEM((2, 4, lat_cols, half), low),
            pltpu.VMEM((4, lat_cols, half), low),
            pltpu.VMEM((4, lat_cols, half), full),
            pltpu.VMEM((4, lat_cols, half), low),
            pltpu.VMEM((depth, 4, lat_cols // depth, half), low),
            pltpu.VMEM((2 * depth, 2, lat_cols // ROW_PARTS // depth, half), low),
            pltpu.VMEM((2, 4, lat_cols, half), low),
            dma((3,)), dma((2,)),
            dma((pieces,)), dma((pieces,)), dma((pieces,)), dma((pieces,)),
            dma((units,)), dma((units,)),
            dma((units, depth)), dma((units, depth)),
            dma((units, depth)), dma((units, depth)),
            dma((units,)), dma((units,)),
            dma((2 * depth,)), dma((2 * depth,)), dma((2 * depth,)), dma((2 * depth,)),
        ],
        compiler_params=pltpu.CompilerParams(
            collective_id=0, has_side_effects=True, vmem_limit_bytes=48 * 2**20
        ),
        name="gradient_sums",
    )(lengths, latent, value_grad)
    return newton_schulz(sums.reshape(width // V_DIM, KV_RANK, V_DIM))


def solution(mesh):
    n_dp, n_head = mesh.shape["dp"], mesh.shape["head"]
    depth = n_dp // 2
    fits = n_head == 4 and KV_RANK // n_head == 16 * ROW_PARTS * depth
    body = functools.partial(kernel_body, depth) if fits else plain_body
    return jax.shard_map(
        body,
        mesh=mesh,
        in_specs=(P("dp", "head"), P("dp", "head"), P()),
        out_specs=P("head", None, None),
        check_vma=False,
    )
```

```python
import functools

import jax
import jax.numpy as jnp
from jax import lax
from jax.experimental import pallas as pl
from jax.experimental.pallas import tpu as pltpu
from jax.sharding import PartitionSpec as P

KV_RANK = 512
V_DIM = 128
ITERS = 5
ROW_PARTS = 2
TOKEN_PARTS = 3

epsilon = 1e-07
coef_one = 3.4445
coef_two = -4.775
coef_three = 2.0315


def plain_body(latent, value_grad, lengths):
    capacity, lat_cols = latent.shape
    grad_width = value_grad.shape[1]
    head_count = grad_width // V_DIM
    my_index = lax.axis_index("dp")
    own_length = lengths[my_index]
    slot_live = jnp.arange(capacity, dtype=jnp.int32) < own_length
    rows_grad = jnp.where(slot_live[:, None], value_grad, jnp.zeros_like(value_grad))
    partial_sum = lax.dot_general(
        lax.all_gather(latent, "head", axis=1, tiled=True),
        rows_grad,
        (((0,), (0,)), ((), ())),
        preferred_element_type=jnp.float32,
    )
    dw_shard = lax.psum_scatter(partial_sum, "dp", scatter_dimension=0, tiled=True)
    shard_heads = dw_shard.reshape(dw_shard.shape[0], head_count, V_DIM)
    local_squares = jnp.sum(shard_heads * shard_heads, axis=(0, 2))
    square_total = lax.psum(local_squares, "dp")
    head_norm = jnp.sqrt(square_total)
    ortho_shard = (shard_heads / (head_norm[None, :, None] + epsilon)).astype(jnp.bfloat16)
    ortho = lax.all_gather(ortho_shard, "dp", axis=0, tiled=True)
    for step in range(ITERS):
        gram_mat = jnp.einsum(
            "rhv,rhw->hvw", ortho, ortho, preferred_element_type=jnp.float32
        ).astype(jnp.bfloat16)
        squared = jnp.einsum("hvu,huw->hvw", gram_mat, gram_mat, preferred_element_type=jnp.float32)
        poly_mat = (coef_two * gram_mat.astype(jnp.float32) + coef_three * squared).astype(
            jnp.bfloat16
        )
        product = jnp.einsum("rhv,hvw->rhw", ortho, poly_mat, preferred_element_type=jnp.float32)
        ortho = (coef_one * ortho.astype(jnp.float32) + product).astype(jnp.bfloat16)
    scale = 0.2 * max(KV_RANK, V_DIM) ** 0.5
    update = (scale * ortho.astype(jnp.float32)).astype(jnp.bfloat16)
    return jnp.transpose(update, (1, 0, 2))


def dot_f32(a, b, dims):
    return lax.dot_general(a, b, (dims, ((), ())), preferred_element_type=jnp.float32)


def newton_schulz(grads):
    wide = grads.astype(jnp.float32)
    inv = 1.0 / (jnp.sqrt(jnp.sum(wide * wide, axis=(1, 2), keepdims=True)) + epsilon)
    ortho = grads
    for step in range(ITERS):
        gram = jnp.einsum("hrv,hrw->hvw", ortho, ortho, preferred_element_type=jnp.float32)
        if step == 0:
            gram = gram * inv * inv
        gram = gram.astype(jnp.bfloat16)
        squared = jnp.einsum("hvu,huw->hvw", gram, gram, preferred_element_type=jnp.float32)
        poly = (coef_two * gram.astype(jnp.float32) + coef_three * squared).astype(jnp.bfloat16)
        product = jnp.einsum("hrv,hvw->hrw", ortho, poly, preferred_element_type=jnp.float32)
        wide = coef_one * ortho.astype(jnp.float32) + product
        if step == 0:
            wide = wide * inv
        ortho = wide.astype(jnp.bfloat16)
    scale = 0.2 * max(KV_RANK, V_DIM) ** 0.5
    return (scale * ortho.astype(jnp.float32)).astype(jnp.bfloat16)


def kernel(
    depth,
    len_hbm, lat_hbm, vg_hbm, out_ref,
    len_s, lat_v, vg_v, lat_t, acc, part, ybuf, zacc, zpart, zbuf, dbuf, grad,
    load_sem, sib_sem, x_send, x_recv, f_send, f_recv,
    y_send, y_recv, z_send, z_recv, a_send, a_recv, b_send, b_recv,
    d_send, d_recv, e_send, e_recv,
):
    dp = lax.axis_index("dp")
    head = lax.axis_index("head")
    y, z = lax.rem(dp, 2), lax.div(dp, 2)
    core = lax.rem(head, 2)
    sibling = head + 1 - 2 * core
    partner = lax.rem(head + 2, 4)
    far = lax.rem(sibling + 2, 4)
    source = (head, sibling, partner, far)
    across = dp + 1 - 2 * y
    lat_cols, capacity = lat_t.shape[1], lat_t.shape[2]
    half = acc.shape[3]
    count = half // V_DIM
    part_rows = lat_cols // ROW_PARTS
    tail = capacity // 6
    span = (capacity - tail) // (TOKEN_PARTS - 1)

    def along(d):
        return lax.rem(z + d, depth) * 2 + y

    def cut(k):
        return pl.ds(k * span, span if k < TOKEN_PARTS - 1 else tail)

    def side(far_y):
        return 1 - y if far_y else y

    def other_dp(far_y, d):
        return lax.rem(z + d, depth) * 2 + side(far_y)

    loads = [
        pltpu.make_async_copy(src, dst, load_sem.at[i])
        for i, (src, dst) in enumerate(((lat_hbm, lat_v), (len_hbm, len_s), (vg_hbm, vg_v)))
    ]
    for c in loads:
        c.start()

    barrier = pltpu.get_barrier_semaphore()
    others = [(far_y, d) for far_y in range(2) for d in range(depth) if far_y or d]
    friends = [(dp, sibling), (dp, partner)]
    friends += [(other_dp(*o), head) for o in others]
    for where in friends:
        pl.semaphore_signal(barrier, inc=1, device_id=where, device_id_type=pl.DeviceIdType.MESH)

    loads[0].wait()
    loads[1].wait()

    def turn(k):
        tokens = cut(k)
        turned = lat_v[tokens, :].T
        live = lax.broadcasted_iota(jnp.int32, turned.shape, 1) + k * span < len_s[dp]
        lat_t[0, :, tokens] = jnp.where(live, turned, jnp.zeros_like(turned))

    turn(0)
    pl.semaphore_wait(barrier, len(friends))

    def remote(src, dst, ssem, rsem, where):
        return pltpu.make_async_remote_copy(
            src_ref=src, dst_ref=dst, send_sem=ssem, recv_sem=rsem,
            device_id=where, device_id_type=pl.DeviceIdType.MESH,
        )

    pieces = [(c, k) for c in range(ROW_PARTS) for k in range(TOKEN_PARTS)]

    def piece(slot, i):
        c, k = pieces[i]
        return lat_t.at[slot, pl.ds(c * part_rows, part_rows), cut(k)]

    over = [
        remote(piece(0, i), piece(2, i), x_send.at[i], x_recv.at[i], (dp, partner))
        for i in range(len(pieces))
    ]
    forward = [
        remote(piece(2, i), piece(3, i), f_send.at[i], f_recv.at[i], (dp, sibling))
        for i in range(len(pieces))
    ]
    near = remote(lat_t.at[0], lat_t.at[1], sib_sem.at[0], sib_sem.at[1], (dp, sibling))
    over[0].start()
    for k in range(1, TOKEN_PARTS):
        turn(k)
    near.start()
    for c in over[1:]:
        c.start()

    own, other = head - core, partner - core
    units = [(own, 0, lat_cols)]
    units += [(other, c * part_rows, part_rows) for c in range(ROW_PARTS)]

    def rows_of(u):
        s, row, rows = units[u]
        return pl.ds(s, 2), pl.ds(row, rows)

    def block_of(u, zz):
        s, row, rows = units[u]
        block = rows // depth
        return pl.ds(s, 2), pl.ds(pl.multiple_of(row + zz * block, block), block)

    def buffer_of(u):
        s, row, rows = units[u]
        return pl.ds(s, 2), pl.ds(row // depth, rows // depth)

    def swap(u):
        slots, here = rows_of(u)
        return remote(
            part.at[1 - y, slots, here], ybuf.at[slots, here],
            y_send.at[u], y_recv.at[u], (across, head),
        )

    def scatter(u, d):
        return remote(
            zpart.at[block_of(u, lax.rem(z + d, depth))], zbuf.at[(d,) + buffer_of(u)],
            z_send.at[u, d], z_recv.at[u, d], (along(d), head),
        )

    def gather(u, d):
        block = grad.at[(y,) + block_of(u, z)]
        return remote(block, block, a_send.at[u, d], a_recv.at[u, d], (along(d), head))

    def share(u):
        block = grad.at[(y,) + rows_of(u)]
        return remote(block, block, b_send.at[u], b_recv.at[u], (across, head))

    def scatter_all(u, far_y, d):
        i = far_y * depth + d
        return remote(
            part.at[(side(far_y),) + block_of(u, lax.rem(z + d, depth))], dbuf.at[i],
            d_send.at[i], d_recv.at[i], (other_dp(far_y, d), head),
        )

    def gather_all(u, far_y, d):
        i = far_y * depth + d
        block = grad.at[(y,) + block_of(u, z)]
        return remote(block, block, e_send.at[i], e_recv.at[i], (other_dp(far_y, d), head))

    def multiply(s, row, rows, k=None):
        tokens = pl.ds(0, capacity) if k is None else cut(k)
        here = pl.ds(row, rows)
        lhs = jnp.concatenate([lat_t[i, here, tokens] for i in s], axis=0)
        for j in range(2):
            value = dot_f32(lhs, vg_v[tokens, pl.ds(j * half, half)], ((1,), (0,)))
            for n, i in enumerate(s):
                mine = value[n * rows : (n + 1) * rows]
                if k:
                    mine = mine + acc[j, source[i], here, :]
                acc[j, source[i], here, :] = mine
                if k is None or k == TOKEN_PARTS - 1:
                    part[j, source[i], here, :] = mine.astype(jnp.bfloat16)

    def stage_z(u):
        here = rows_of(u)
        swap(u).wait_recv()
        total = acc[(y,) + here] + ybuf[here].astype(jnp.float32)
        zacc[here] = total
        zpart[here] = total.astype(jnp.bfloat16)
        for d in range(1, depth):
            scatter(u, d).start()

    def stage_gather(u):
        total = zacc[block_of(u, z)]
        for d in range(1, depth):
            scatter(u, d).wait_recv()
            total = total + zbuf[(d,) + buffer_of(u)].astype(jnp.float32)
        keep(u, total)
        for d in range(1, depth):
            gather(u, d).start()

    def keep(u, total):
        grad[(y,) + block_of(u, z)] = total.astype(jnp.bfloat16)

    def reduce_all(u):
        total = acc[(y,) + block_of(u, z)]
        for o in others:
            scatter_all(u, *o).wait_recv()
            total = total + dbuf[o[0] * depth + o[1]].astype(jnp.float32)
        keep(u, total)
        for o in others:
            gather_all(u, *o).start()

    def stage_share(u):
        for d in range(1, depth):
            gather(u, d).wait_recv()
        share(u).start()

    def arrive(i):
        over[i].wait_recv()
        forward[i].start()

    last = len(units) - 1
    loads[2].wait()
    multiply([0], 0, lat_cols)
    near.wait_recv()
    multiply([1], 0, lat_cols)
    swap(0).start()

    def multiply_piece(i):
        c, k = pieces[i]
        forward[i].wait_recv()
        multiply([2, 3], c * part_rows, part_rows, k)
        if i == TOKEN_PARTS - 1:
            swap(1).start()

    arrive(0)
    for i in range(1, len(pieces)):
        arrive(i)
        if i == 1:
            stage_z(0)
        if i == len(pieces) - 1:
            stage_z(1)
        multiply_piece(i - 1)
        if i == TOKEN_PARTS:
            stage_gather(0)
    multiply_piece(len(pieces) - 1)
    for o in others:
        scatter_all(last, *o).start()
    stage_share(0)
    stage_gather(1)
    reduce_all(last)
    stage_share(1)
    for u in range(last):
        share(u).wait_recv()
    for o in others:
        gather_all(last, *o).wait_recv()
    for j in range(2):
        for h in range(count):
            out_ref[j * count + h] = grad[j, :, :, pl.ds(h * V_DIM, V_DIM)]

    near.wait_send()
    for i in range(len(pieces)):
        over[i].wait_send()
        forward[i].wait_send()
    for o in others:
        scatter_all(last, *o).wait_send()
        gather_all(last, *o).wait_send()
    for u in range(last):
        swap(u).wait_send()
        share(u).wait_send()
        for d in range(1, depth):
            scatter(u, d).wait_send()
            gather(u, d).wait_send()


def kernel_body(depth, latent, value_grad, lengths):
    capacity, lat_cols = latent.shape
    width = value_grad.shape[1]
    half = width // 2
    units, pieces = ROW_PARTS, ROW_PARTS * TOKEN_PARTS
    dma = pltpu.SemaphoreType.DMA
    low, full = jnp.bfloat16, jnp.float32
    latent, value_grad, lengths = (
        pltpu.with_memory_space_constraint(a, pltpu.HBM) for a in (latent, value_grad, lengths)
    )
    sums = pl.pallas_call(
        functools.partial(kernel, depth),
        out_shape=pltpu.VMEM((width // V_DIM, 4, lat_cols, V_DIM), low),
        in_specs=[pl.BlockSpec(memory_space=pltpu.HBM)] * 3,
        out_specs=pl.BlockSpec(memory_space=pltpu.VMEM),
        scratch_shapes=[
            pltpu.SMEM(lengths.shape, jnp.int32),
            pltpu.VMEM((capacity, lat_cols), low),
            pltpu.VMEM((capacity, width), low),
            pltpu.VMEM((4, lat_cols, capacity), low),
            pltpu.VMEM((2, 4, lat_cols, half), full),
            pltpu.VMEM((2, 4, lat_cols, half), low),
            pltpu.VMEM((4, lat_cols, half), low),
            pltpu.VMEM((4, lat_cols, half), full),
            pltpu.VMEM((4, lat_cols, half), low),
            pltpu.VMEM((depth, 4, lat_cols // depth, half), low),
            pltpu.VMEM((2 * depth, 2, lat_cols // ROW_PARTS // depth, half), low),
            pltpu.VMEM((2, 4, lat_cols, half), low),
            dma((3,)), dma((2,)),
            dma((pieces,)), dma((pieces,)), dma((pieces,)), dma((pieces,)),
            dma((units,)), dma((units,)),
            dma((units, depth)), dma((units, depth)),
            dma((units, depth)), dma((units, depth)),
            dma((units,)), dma((units,)),
            dma((2 * depth,)), dma((2 * depth,)), dma((2 * depth,)), dma((2 * depth,)),
        ],
        compiler_params=pltpu.CompilerParams(
            collective_id=0, has_side_effects=True, vmem_limit_bytes=48 * 2**20
        ),
        name="gradient_sums",
    )(lengths, latent, value_grad)
    return newton_schulz(sums.reshape(width // V_DIM, KV_RANK, V_DIM))


def solution(mesh):
    n_dp, n_head = mesh.shape["dp"], mesh.shape["head"]
    depth = n_dp // 2
    fits = n_head == 4 and KV_RANK // n_head == 16 * ROW_PARTS * depth
    body = functools.partial(kernel_body, depth) if fits else plain_body
    return jax.shard_map(
        body,
        mesh=mesh,
        in_specs=(P("dp", "head"), P("dp", "head"), P()),
        out_specs=P("head", None, None),
        check_vma=False,
    )
```

```python
import functools

import jax
import jax.numpy as jnp
from jax import lax
from jax.experimental import pallas as pl
from jax.experimental.pallas import tpu as pltpu
from jax.sharding import PartitionSpec as P

KV_RANK = 512
V_DIM = 128
ITERS = 5
ROW_PARTS = 2
TOKEN_PARTS = 3

epsilon = 1e-07
coef_one = 3.4445
coef_two = -4.775
coef_three = 2.0315


def plain_body(latent, value_grad, lengths):
    capacity, lat_cols = latent.shape
    grad_width = value_grad.shape[1]
    head_count = grad_width // V_DIM
    my_index = lax.axis_index("dp")
    own_length = lengths[my_index]
    slot_live = jnp.arange(capacity, dtype=jnp.int32) < own_length
    rows_grad = jnp.where(slot_live[:, None], value_grad, jnp.zeros_like(value_grad))
    partial_sum = lax.dot_general(
        lax.all_gather(latent, "head", axis=1, tiled=True),
        rows_grad,
        (((0,), (0,)), ((), ())),
        preferred_element_type=jnp.float32,
    )
    dw_shard = lax.psum_scatter(partial_sum, "dp", scatter_dimension=0, tiled=True)
    shard_heads = dw_shard.reshape(dw_shard.shape[0], head_count, V_DIM)
    local_squares = jnp.sum(shard_heads * shard_heads, axis=(0, 2))
    square_total = lax.psum(local_squares, "dp")
    head_norm = jnp.sqrt(square_total)
    ortho_shard = (shard_heads / (head_norm[None, :, None] + epsilon)).astype(jnp.bfloat16)
    ortho = lax.all_gather(ortho_shard, "dp", axis=0, tiled=True)
    for step in range(ITERS):
        gram_mat = jnp.einsum(
            "rhv,rhw->hvw", ortho, ortho, preferred_element_type=jnp.float32
        ).astype(jnp.bfloat16)
        squared = jnp.einsum("hvu,huw->hvw", gram_mat, gram_mat, preferred_element_type=jnp.float32)
        poly_mat = (coef_two * gram_mat.astype(jnp.float32) + coef_three * squared).astype(
            jnp.bfloat16
        )
        product = jnp.einsum("rhv,hvw->rhw", ortho, poly_mat, preferred_element_type=jnp.float32)
        ortho = (coef_one * ortho.astype(jnp.float32) + product).astype(jnp.bfloat16)
    scale = 0.2 * max(KV_RANK, V_DIM) ** 0.5
    update = (scale * ortho.astype(jnp.float32)).astype(jnp.bfloat16)
    return jnp.transpose(update, (1, 0, 2))


def dot_f32(a, b, dims):
    return lax.dot_general(a, b, (dims, ((), ())), preferred_element_type=jnp.float32)


def newton_schulz(grads):
    wide = grads.astype(jnp.float32)
    inv = 1.0 / (jnp.sqrt(jnp.sum(wide * wide, axis=(1, 2), keepdims=True)) + epsilon)
    ortho = grads
    for step in range(ITERS):
        gram = jnp.einsum("hrv,hrw->hvw", ortho, ortho, preferred_element_type=jnp.float32)
        if step == 0:
            gram = gram * inv * inv
        gram = gram.astype(jnp.bfloat16)
        squared = jnp.einsum("hvu,huw->hvw", gram, gram, preferred_element_type=jnp.float32)
        poly = (coef_two * gram.astype(jnp.float32) + coef_three * squared).astype(jnp.bfloat16)
        product = jnp.einsum("hrv,hvw->hrw", ortho, poly, preferred_element_type=jnp.float32)
        wide = coef_one * ortho.astype(jnp.float32) + product
        if step == 0:
            wide = wide * inv
        ortho = wide.astype(jnp.bfloat16)
    scale = 0.2 * max(KV_RANK, V_DIM) ** 0.5
    return (scale * ortho.astype(jnp.float32)).astype(jnp.bfloat16)


def kernel(
    depth,
    len_hbm, lat_hbm, vg_hbm, out_ref,
    len_s, lat_v, vg_v, lat_t, acc, part, ybuf, zacc, zpart, zbuf, dbuf, grad,
    load_sem, sib_sem, x_send, x_recv, f_send, f_recv,
    y_send, y_recv, z_send, z_recv, a_send, a_recv, b_send, b_recv,
    d_send, d_recv, e_send, e_recv,
):
    dp = lax.axis_index("dp")
    head = lax.axis_index("head")
    y, z = lax.rem(dp, 2), lax.div(dp, 2)
    core = lax.rem(head, 2)
    sibling = head + 1 - 2 * core
    partner = lax.rem(head + 2, 4)
    far = lax.rem(sibling + 2, 4)
    source = (head, sibling, partner, far)
    across = dp + 1 - 2 * y
    lat_cols, capacity = lat_t.shape[1], lat_t.shape[2]
    half = acc.shape[3]
    count = half // V_DIM
    part_rows = lat_cols // ROW_PARTS
    tail = capacity // 6
    span = (capacity - tail) // (TOKEN_PARTS - 1)

    def along(d):
        return lax.rem(z + d, depth) * 2 + y

    def cut(k):
        return pl.ds(k * span, span if k < TOKEN_PARTS - 1 else tail)

    def side(far_y):
        return 1 - y if far_y else y

    def other_dp(far_y, d):
        return lax.rem(z + d, depth) * 2 + side(far_y)

    loads = [
        pltpu.make_async_copy(src, dst, load_sem.at[i])
        for i, (src, dst) in enumerate(((lat_hbm, lat_v), (len_hbm, len_s), (vg_hbm, vg_v)))
    ]
    for c in loads:
        c.start()

    barrier = pltpu.get_barrier_semaphore()
    others = [(far_y, d) for far_y in range(2) for d in range(depth) if far_y or d]
    friends = [(dp, sibling), (dp, partner)]
    friends += [(other_dp(*o), head) for o in others]
    for where in friends:
        pl.semaphore_signal(barrier, inc=1, device_id=where, device_id_type=pl.DeviceIdType.MESH)

    loads[0].wait()
    loads[1].wait()

    def turn(k):
        tokens = cut(k)
        turned = lat_v[tokens, :].T
        live = lax.broadcasted_iota(jnp.int32, turned.shape, 1) + k * span < len_s[dp]
        lat_t[0, :, tokens] = jnp.where(live, turned, jnp.zeros_like(turned))

    turn(0)
    pl.semaphore_wait(barrier, len(friends))

    def remote(src, dst, ssem, rsem, where):
        return pltpu.make_async_remote_copy(
            src_ref=src, dst_ref=dst, send_sem=ssem, recv_sem=rsem,
            device_id=where, device_id_type=pl.DeviceIdType.MESH,
        )

    pieces = [(c, k) for c in range(ROW_PARTS) for k in range(TOKEN_PARTS)]

    def piece(slot, i):
        c, k = pieces[i]
        return lat_t.at[slot, pl.ds(c * part_rows, part_rows), cut(k)]

    over = [
        remote(piece(0, i), piece(2, i), x_send.at[i], x_recv.at[i], (dp, partner))
        for i in range(len(pieces))
    ]
    forward = [
        remote(piece(2, i), piece(3, i), f_send.at[i], f_recv.at[i], (dp, sibling))
        for i in range(len(pieces))
    ]
    near = remote(lat_t.at[0], lat_t.at[1], sib_sem.at[0], sib_sem.at[1], (dp, sibling))
    over[0].start()
    for k in range(1, TOKEN_PARTS):
        turn(k)
    near.start()
    for c in over[1:]:
        c.start()

    own, other = head - core, partner - core
    units = [(own, 0, lat_cols)]
    units += [(other, c * part_rows, part_rows) for c in range(ROW_PARTS)]

    def rows_of(u):
        s, row, rows = units[u]
        return pl.ds(s, 2), pl.ds(row, rows)

    def block_of(u, zz):
        s, row, rows = units[u]
        block = rows // depth
        return pl.ds(s, 2), pl.ds(pl.multiple_of(row + zz * block, block), block)

    def buffer_of(u):
        s, row, rows = units[u]
        return pl.ds(s, 2), pl.ds(row // depth, rows // depth)

    def swap(u):
        slots, here = rows_of(u)
        return remote(
            part.at[1 - y, slots, here], ybuf.at[slots, here],
            y_send.at[u], y_recv.at[u], (across, head),
        )

    def scatter(u, d):
        return remote(
            zpart.at[block_of(u, lax.rem(z + d, depth))], zbuf.at[(d,) + buffer_of(u)],
            z_send.at[u, d], z_recv.at[u, d], (along(d), head),
        )

    def gather(u, d):
        block = grad.at[(y,) + block_of(u, z)]
        return remote(block, block, a_send.at[u, d], a_recv.at[u, d], (along(d), head))

    def share(u):
        block = grad.at[(y,) + rows_of(u)]
        return remote(block, block, b_send.at[u], b_recv.at[u], (across, head))

    def scatter_all(u, far_y, d):
        i = far_y * depth + d
        return remote(
            part.at[(side(far_y),) + block_of(u, lax.rem(z + d, depth))], dbuf.at[i],
            d_send.at[i], d_recv.at[i], (other_dp(far_y, d), head),
        )

    def gather_all(u, far_y, d):
        i = far_y * depth + d
        block = grad.at[(y,) + block_of(u, z)]
        return remote(block, block, e_send.at[i], e_recv.at[i], (other_dp(far_y, d), head))

    def multiply(s, row, rows, k=None):
        tokens = pl.ds(0, capacity) if k is None else cut(k)
        here = pl.ds(row, rows)
        lhs = jnp.concatenate([lat_t[i, here, tokens] for i in s], axis=0)
        for j in range(2):
            value = dot_f32(lhs, vg_v[tokens, pl.ds(j * half, half)], ((1,), (0,)))
            for n, i in enumerate(s):
                mine = value[n * rows : (n + 1) * rows]
                if k:
                    mine = mine + acc[j, source[i], here, :]
                acc[j, source[i], here, :] = mine
                if k is None or k == TOKEN_PARTS - 1:
                    part[j, source[i], here, :] = mine.astype(jnp.bfloat16)

    def stage_z(u):
        here = rows_of(u)
        swap(u).wait_recv()
        total = acc[(y,) + here] + ybuf[here].astype(jnp.float32)
        zacc[here] = total
        zpart[here] = total.astype(jnp.bfloat16)
        for d in range(1, depth):
            scatter(u, d).start()

    def stage_gather(u):
        total = zacc[block_of(u, z)]
        for d in range(1, depth):
            scatter(u, d).wait_recv()
            total = total + zbuf[(d,) + buffer_of(u)].astype(jnp.float32)
        keep(u, total)
        for d in range(1, depth):
            gather(u, d).start()

    def keep(u, total):
        grad[(y,) + block_of(u, z)] = total.astype(jnp.bfloat16)

    def reduce_all(u):
        total = acc[(y,) + block_of(u, z)]
        for o in others:
            scatter_all(u, *o).wait_recv()
            total = total + dbuf[o[0] * depth + o[1]].astype(jnp.float32)
        keep(u, total)
        for o in others:
            gather_all(u, *o).start()

    def stage_share(u):
        for d in range(1, depth):
            gather(u, d).wait_recv()
        share(u).start()

    def arrive(i):
        over[i].wait_recv()
        forward[i].start()

    last = len(units) - 1
    loads[2].wait()
    multiply([0], 0, lat_cols)
    near.wait_recv()
    multiply([1], 0, lat_cols)
    swap(0).start()

    def multiply_piece(i):
        c, k = pieces[i]
        forward[i].wait_recv()
        multiply([2, 3], c * part_rows, part_rows, k)
        if i == TOKEN_PARTS - 1:
            swap(1).start()

    arrive(0)
    for i in range(1, len(pieces)):
        arrive(i)
        if i == 1:
            stage_z(0)
        if i == len(pieces) - 1:
            stage_z(1)
        multiply_piece(i - 1)
        if i == TOKEN_PARTS:
            stage_gather(0)
    stage_share(0)
    multiply_piece(len(pieces) - 1)
    for o in others:
        scatter_all(last, *o).start()
    stage_gather(1)
    reduce_all(last)
    stage_share(1)
    for u in range(last):
        share(u).wait_recv()
    for o in others:
        gather_all(last, *o).wait_recv()
    for j in range(2):
        for h in range(count):
            out_ref[j * count + h] = grad[j, :, :, pl.ds(h * V_DIM, V_DIM)]

    near.wait_send()
    for i in range(len(pieces)):
        over[i].wait_send()
        forward[i].wait_send()
    for o in others:
        scatter_all(last, *o).wait_send()
        gather_all(last, *o).wait_send()
    for u in range(last):
        swap(u).wait_send()
        share(u).wait_send()
        for d in range(1, depth):
            scatter(u, d).wait_send()
            gather(u, d).wait_send()


def kernel_body(depth, latent, value_grad, lengths):
    capacity, lat_cols = latent.shape
    width = value_grad.shape[1]
    half = width // 2
    units, pieces = ROW_PARTS, ROW_PARTS * TOKEN_PARTS
    dma = pltpu.SemaphoreType.DMA
    low, full = jnp.bfloat16, jnp.float32
    latent, value_grad, lengths = (
        pltpu.with_memory_space_constraint(a, pltpu.HBM) for a in (latent, value_grad, lengths)
    )
    sums = pl.pallas_call(
        functools.partial(kernel, depth),
        out_shape=pltpu.VMEM((width // V_DIM, 4, lat_cols, V_DIM), low),
        in_specs=[pl.BlockSpec(memory_space=pltpu.HBM)] * 3,
        out_specs=pl.BlockSpec(memory_space=pltpu.VMEM),
        scratch_shapes=[
            pltpu.SMEM(lengths.shape, jnp.int32),
            pltpu.VMEM((capacity, lat_cols), low),
            pltpu.VMEM((capacity, width), low),
            pltpu.VMEM((4, lat_cols, capacity), low),
            pltpu.VMEM((2, 4, lat_cols, half), full),
            pltpu.VMEM((2, 4, lat_cols, half), low),
            pltpu.VMEM((4, lat_cols, half), low),
            pltpu.VMEM((4, lat_cols, half), full),
            pltpu.VMEM((4, lat_cols, half), low),
            pltpu.VMEM((depth, 4, lat_cols // depth, half), low),
            pltpu.VMEM((2 * depth, 2, lat_cols // ROW_PARTS // depth, half), low),
            pltpu.VMEM((2, 4, lat_cols, half), low),
            dma((3,)), dma((2,)),
            dma((pieces,)), dma((pieces,)), dma((pieces,)), dma((pieces,)),
            dma((units,)), dma((units,)),
            dma((units, depth)), dma((units, depth)),
            dma((units, depth)), dma((units, depth)),
            dma((units,)), dma((units,)),
            dma((2 * depth,)), dma((2 * depth,)), dma((2 * depth,)), dma((2 * depth,)),
        ],
        compiler_params=pltpu.CompilerParams(
            collective_id=0, has_side_effects=True, vmem_limit_bytes=48 * 2**20
        ),
        name="gradient_sums",
    )(lengths, latent, value_grad)
    return newton_schulz(sums.reshape(width // V_DIM, KV_RANK, V_DIM))


def solution(mesh):
    n_dp, n_head = mesh.shape["dp"], mesh.shape["head"]
    depth = n_dp // 2
    fits = n_head == 4 and KV_RANK // n_head == 16 * ROW_PARTS * depth
    body = functools.partial(kernel_body, depth) if fits else plain_body
    return jax.shard_map(
        body,
        mesh=mesh,
        in_specs=(P("dp", "head"), P("dp", "head"), P()),
        out_specs=P("head", None, None),
        check_vma=False,
    )
```
